128 devices in a mesh: grp: 8 (over x, y_hi), head: 16 (over z, y_lo, core).
Axes of the slice: x: 4, y: 4 (y_hi: 2, y_lo: 2; y = y_hi * 2 + y_lo), z: 4, core: 2. Of those that a mesh axis runs over, the one named last changes fastest.
Arguments:
- hidden_in: bfloat16 [128, 8192], replicated, may hold values from -6 to 6
- row_owner: int32 [128], replicated, may hold values from 0 to 15, as said below
- history_len: int32 [128], replicated, may hold values from 0 to 3
- pre_gain: bfloat16 [8192], replicated, may hold values from 0.099609375 to 1.8984375
- inner_proj: bfloat16 [8192, 2, 16384], P('head', None, 'grp'), may hold values from -0.0625 to 0.0625
- select_proj: bfloat16 [8192, 2, 1024], P('head', None, 'grp'), may hold values from -0.0625 to 0.0625
- step_proj: bfloat16 [8192, 256], P('head', 'grp'), may hold values from -0.0625 to 0.0625
- step_bias: float32 [256], P('grp'), may hold values from -4 to -1
- decay_log: float32 [256], P('grp'), may hold values from -1 to 2
- skip_gain: float32 [256], P('grp'), may hold values from 0.5 to 1.5
- conv_taps: bfloat16 [5, 8, 2304], P(None, 'grp'), may hold values from -3 to 3
- conv_window: bfloat16 [128, 3, 8, 2304], P('head', None, 'grp'), may hold values from -6 to 6
- state_cache: bfloat16 [128, 256, 64, 128], P('head', 'grp'), may hold values from -6 to 6
- mixer_gain: bfloat16 [8, 2048], P('grp'), may hold values from 0.099609375 to 1.8984375
- output_proj: bfloat16 [8, 2048, 8192], P('grp', None, 'head'), may hold values from -0.046875 to 0.046875
- channel_gain: bfloat16 [8192], replicated, may hold values from 0.099609375 to 1.8984375
- up_weight: bfloat16 [8192, 32768], P(None, ('grp', 'head')), may hold values from -0.0625 to 0.0625
- down_weight: bfloat16 [32768, 8192], P(('grp', 'head')), may hold values from -0.125 to 0.125
Outputs:
- block_out: bfloat16 [128, 8192], P(None, ('grp', 'head'))
- state_next: bfloat16 [128, 256, 64, 128], P('head', 'grp')
- window_next: bfloat16 [128, 3, 8, 2304], P('head', None, 'grp')
The draws below stay inside these ranges and needn't reach their ends.
Inputs may be any that keep to these rules, and one draw needn't show every extreme that they name: Every owner is named by exactly 8 rows. Block h of 8 slots of state_cache, conv_window, state_next and window_next belongs to the rows that row_owner assigns to h, in increasing row order.
All inputs are finite; a program needn't handle non-finite values.
Results may differ from the reference program's by a relative error of at most 0.023.
Values may be sent and summed in bfloat16 or wider, within the bound.
No kernel may reach another device: no remote copies, remote signals or barrier semaphores. Data moves between devices by JAX's collectives and lax.ppermute only.
A program may use at most 128 MiB of HBM per device.

```python
import jax
import jax.numpy as jnp
from jax import lax

D = 8192
MIX_HEADS = 256
HEAD_DIM = 64
STATE = 128
GROUPS = 8
CONV_K = 4
FF = 32768
ROWS_OWN = 8
ROWS = 128
D_INNER = 16384
CH_GRP = 2048


def draw_row_owner(key, part):
    key = jax.random.fold_in(key, 11)
    labels = jnp.arange(ROWS, dtype=jnp.int32) // ROWS_OWN
    return jax.random.permutation(key, labels).astype(jnp.int32)


def touch_ends(drawn, stream_key, least, top_value):
    index_at = [jax.random.randint(jax.random.fold_in(stream_key, axis), (), 0, length) for axis, length in enumerate(drawn.shape)]
    widest = drawn.shape.index(max(drawn.shape))
    next_to = index_at[:widest] + [(index_at[widest] + 1) % drawn.shape[widest]] + index_at[widest + 1:]
    return drawn.at[tuple(index_at)].set(least).at[tuple(next_to)].set(top_value)


def with_spikes(entries, rng, source, target, shards_of, factor):
    def block_of(axis_at):
        return (jnp.arange(entries.shape[axis_at]) // (entries.shape[axis_at] // shards_of)).reshape((-1,) + (1,) * (entries.ndim - 1 - axis_at))

    first = jax.random.permutation(rng, shards_of)[block_of(target)]
    far = (block_of(target) + shards_of // 2) % shards_of
    return jnp.where((block_of(source) == first) | (block_of(source) == far), factor * entries, entries)


def level_of(rng, shape, pieces, low, high):
    level = 1.0
    for dim, blocks in pieces:
        steps = jax.random.uniform(jax.random.fold_in(jax.random.fold_in(rng, 6), dim), (blocks,), jnp.float32, low / len(pieces), high / len(pieces))
        level = level * jnp.repeat(jnp.exp(steps), shape[dim] // blocks).reshape((-1,) + (1,) * (len(shape) - 1 - dim))
    return level


def centred(own_key, shape, width, most, shards=(), held_as=jnp.bfloat16):
    array = width * jax.random.normal(own_key, shape, jnp.float32)
    if shards:
        array = array * level_of(own_key, shape, shards, -0.22, 0.18)
    return jnp.clip(array, -most, most).astype(held_as)


def gaussian_with(own_key, dims, deviation, most, split, heavy, held_as=jnp.bfloat16):
    values = deviation * jax.random.normal(own_key, dims, jnp.float32)
    if split:
        values = values * level_of(own_key, dims, split, -0.22, 0.18)
    return jnp.clip(with_spikes(values, jax.random.fold_in(own_key, 3), *heavy), -most, most).astype(held_as)


def setup_inputs(seed: int = 0) -> dict:
    keys = jax.random.split(jax.random.key(seed), 19)
    hidden_in = centred(keys[0], (ROWS, D), 1.0, 6.0)
    row_owner = draw_row_owner(jax.random.fold_in(keys[18], 71), 0)
    history_len = touch_ends(jax.random.randint(keys[2], (ROWS,), 0, CONV_K), jax.random.fold_in(keys[2], 1), 0, CONV_K - 1).astype(jnp.int32)
    pre_gain = jnp.clip(1.0 + 0.18 * jax.random.normal(keys[3], (D,), jnp.float32), 0.099609375, 1.8984375).astype(jnp.bfloat16)
    inner_proj = centred(keys[4], (D, 2, D_INNER), D ** -0.5, 0.0625, ((0, 16), (2, 8)))
    select_proj = centred(keys[5], (D, 2, GROUPS * STATE), D ** -0.5, 0.0625, ((0, 16), (2, 8)))
    step_proj = centred(keys[6], (D, MIX_HEADS), D ** -0.5, 0.0625, ((0, 16), (1, 8)))
    step_bias = jnp.clip(-4.0 + 3.0 * jax.random.uniform(keys[7], (MIX_HEADS,), jnp.float32) ** level_of(keys[7], (MIX_HEADS,), ((0, 8),), -0.2, 0.2), -4.0, -1.0)
    decay_log = jnp.clip(-1.0 + 3.0 * jax.random.uniform(keys[8], (MIX_HEADS,), jnp.float32) ** level_of(keys[8], (MIX_HEADS,), ((0, 8),), -0.2, 0.2), -1.0, 2.0)
    skip_gain = jnp.clip(0.5 + 1.0 * jax.random.uniform(keys[9], (MIX_HEADS,), jnp.float32) ** level_of(keys[9], (MIX_HEADS,), ((0, 8),), -0.2, 0.2), 0.5, 1.5)
    conv_taps = centred(keys[10], (CONV_K + 1, GROUPS, CH_GRP + 2 * STATE), 0.5, 3.0, ((1, 8),))
    conv_window = centred(keys[11], (ROWS, CONV_K - 1, GROUPS, CH_GRP + 2 * STATE), 1.0, 6.0, ((0, 16), (2, 8)))
    state_cache = centred(keys[12], (ROWS, MIX_HEADS, HEAD_DIM, STATE), 1.0, 6.0, ((0, 16), (1, 8)))
    mixer_gain = jnp.clip(1.0 + 0.18 * jax.random.normal(keys[13], (GROUPS, CH_GRP), jnp.float32), 0.099609375, 1.8984375).astype(jnp.bfloat16)
    output_proj = centred(keys[14], (GROUPS, CH_GRP, D), D_INNER ** -0.5, 0.046875, ((0, 8), (2, 16)))
    channel_gain = jnp.clip(1.0 + 0.18 * jax.random.normal(keys[15], (D,), jnp.float32), 0.099609375, 1.8984375).astype(jnp.bfloat16)
    up_weight = centred(keys[16], (D, FF), D ** -0.5, 0.0625, ((1, 128),))
    down_weight = gaussian_with(keys[17], (FF, D), FF ** -0.5, 0.125, ((0, 128),), (0, 1, 128, 5.5))
    return {"hidden_in": hidden_in, "row_owner": row_owner, "history_len": history_len, "pre_gain": pre_gain, "inner_proj": inner_proj, "select_proj": select_proj, "step_proj": step_proj, "step_bias": step_bias, "decay_log": decay_log, "skip_gain": skip_gain, "conv_taps": conv_taps, "conv_window": conv_window, "state_cache": state_cache, "mixer_gain": mixer_gain, "output_proj": output_proj, "channel_gain": channel_gain, "up_weight": up_weight, "down_weight": down_weight}


EPS = 1e-05
HIGHEST = lax.Precision.HIGHEST

def rms_scale(values):
    return lax.rsqrt(lax.optimization_barrier(jnp.mean(values * values, axis=-1, keepdims=True)) + EPS)

def mixer(inner_terms, select_terms, step_raw, history_slot, step_bias, decay_log, skip_gain, conv_taps, conv_window, state_groups, mixer_gain):
    count_rows = inner_terms.shape[0]
    groups = inner_terms.shape[2]
    channels = inner_terms.shape[3]
    state_size = select_terms.shape[3]
    head_count = state_groups.shape[2]
    head_width = state_groups.shape[3]
    tap_count = conv_taps.shape[0] - 1
    fresh_input = jnp.concatenate([inner_terms[:, 1], select_terms[:, 0], select_terms[:, 1]], axis=-1).astype(jnp.bfloat16)
    window = jnp.concatenate([conv_window, fresh_input[:, None]], axis=1).astype(jnp.float32)
    lag_index = jnp.arange(tap_count, dtype=jnp.int32)
    valid_mask = (lag_index[None, :] >= (tap_count - 1 - history_slot)[:, None]).astype(jnp.float32)
    window = window * valid_mask[:, :, None, None]
    weights = conv_taps.astype(jnp.float32)
    conv_sum = jnp.einsum('rkgc,kgc->rgc', window, weights[:tap_count], precision=HIGHEST) + weights[tap_count]
    activated = jax.nn.silu(conv_sum)
    inputs = activated[..., :channels].reshape(count_rows, groups, head_count, head_width)
    in_coef = activated[..., channels:channels + state_size]
    out_coef = activated[..., channels + state_size:]
    step_size = jax.nn.softplus(step_raw + step_bias.astype(jnp.float32))
    decay_rate = jnp.exp(-step_size * jnp.exp(decay_log.astype(jnp.float32)))
    updated = decay_rate[..., None, None] * state_groups.astype(jnp.float32) + (step_size[..., None] * inputs)[..., None] * in_coef[:, :, None, None, :]
    readout = jnp.einsum('rghpn,rgn->rghp', updated, out_coef, precision=HIGHEST) + skip_gain.astype(jnp.float32)[..., None] * inputs
    gated_out = readout.reshape(count_rows, groups, channels) * jax.nn.silu(inner_terms[:, 0])
    normed = (gated_out * rms_scale(gated_out) * mixer_gain.astype(jnp.float32)).astype(jnp.bfloat16)
    return (normed, updated.astype(jnp.bfloat16), window[:, 1:].astype(jnp.bfloat16))

def reference(hidden_in, row_owner, history_len, pre_gain, inner_proj, select_proj, step_proj, step_bias, decay_log, skip_gain, conv_taps, conv_window, state_cache, mixer_gain, output_proj, channel_gain, up_weight, down_weight):
    total_rows = hidden_in.shape[0]
    per_group = MIX_HEADS // GROUPS
    positions = jnp.arange(total_rows, dtype=jnp.int32)
    slot_order = jnp.argsort(row_owner * total_rows + positions).astype(jnp.int32)
    slot_of_row = jnp.argsort(slot_order).astype(jnp.int32)
    hidden_wide = hidden_in.astype(jnp.float32)
    normed = (hidden_wide * rms_scale(hidden_wide) * pre_gain.astype(jnp.float32)).astype(jnp.bfloat16)
    sorted_rows = normed[slot_order]
    inner_terms = jnp.dot(sorted_rows, inner_proj.reshape(D, 2 * D_INNER), preferred_element_type=jnp.float32).reshape(total_rows, 2, GROUPS, CH_GRP)
    select_terms = jnp.dot(sorted_rows, select_proj.reshape(D, 2 * GROUPS * STATE), preferred_element_type=jnp.float32).reshape(total_rows, 2, GROUPS, STATE)
    step_raw = jnp.dot(sorted_rows, step_proj, preferred_element_type=jnp.float32).reshape(total_rows, GROUPS, per_group)
    history_slot = history_len[slot_order]
    state_groups = state_cache.reshape(total_rows, GROUPS, per_group, HEAD_DIM, STATE)
    bias_groups = step_bias.reshape(GROUPS, per_group)
    decay_groups = decay_log.reshape(GROUPS, per_group)
    skip_groups = skip_gain.reshape(GROUPS, per_group)
    normed_parts = []
    state_parts = []
    window_parts = []
    for group in range(GROUPS):
        upper = group + 1
        result_norm, result_state, result_window = mixer(inner_terms[:, :, group:upper], select_terms[:, :, group:upper], step_raw[:, group:upper], history_slot, bias_groups[group:upper], decay_groups[group:upper], skip_groups[group:upper], conv_taps[:, group:upper], conv_window[:, :, group:upper], state_groups[:, group:upper], mixer_gain[group:upper])
        normed_parts.append(result_norm)
        state_parts.append(result_state)
        window_parts.append(result_window)
    normed_mix = jnp.concatenate(normed_parts, axis=1)
    state_next = jnp.concatenate(state_parts, axis=1).reshape(total_rows, MIX_HEADS, HEAD_DIM, STATE)
    window_next = jnp.concatenate(window_parts, axis=2)
    mixed_rows = jnp.dot(normed_mix.reshape(total_rows, D_INNER), output_proj.reshape(D_INNER, D), preferred_element_type=jnp.float32)
    residual = (hidden_wide + mixed_rows[slot_of_row]).astype(jnp.bfloat16)
    residual_wide = residual.astype(jnp.float32)
    ffn_input = (residual_wide * rms_scale(residual_wide) * channel_gain.astype(jnp.float32)).astype(jnp.bfloat16)
    raised = jnp.maximum(jnp.dot(ffn_input, up_weight, preferred_element_type=jnp.float32), 0.0)
    squared = (raised * raised).astype(jnp.bfloat16)
    block_out = (residual_wide + jnp.dot(squared, down_weight, preferred_element_type=jnp.float32)).astype(jnp.bfloat16)
    return (block_out, state_next, window_next)
```

```python
import jax
import jax.numpy as jnp
from jax import lax
from jax.sharding import Mesh, PartitionSpec as P

EPS = 1e-05
HIGHEST = lax.Precision.HIGHEST
GRP = ("x", "yh")
HEAD = ("z", "yl", "c")
CHIPS = ("x", "yh", "z", "yl")


def rms_scale(values):
    return lax.rsqrt(jnp.mean(values * values, axis=-1, keepdims=True) + EPS)


def swap(value, axis, bit):
    size = lax.axis_size(axis)
    return lax.ppermute(value, axis, [(i, i ^ bit) for i in range(size)])


def mixer(
    inner_terms,
    select_terms,
    step_raw,
    history_slot,
    step_bias,
    decay_log,
    skip_gain,
    conv_taps,
    conv_window,
    state_groups,
    mixer_gain,
):
    count_rows = inner_terms.shape[0]
    groups = inner_terms.shape[2]
    channels = inner_terms.shape[3]
    state_size = select_terms.shape[3]
    head_count = state_groups.shape[2]
    head_width = state_groups.shape[3]
    tap_count = conv_taps.shape[0] - 1
    fresh_input = jnp.concatenate(
        [inner_terms[:, 1], select_terms[:, 0], select_terms[:, 1]], axis=-1
    ).astype(jnp.bfloat16)
    window = jnp.concatenate([conv_window, fresh_input[:, None]], axis=1).astype(jnp.float32)
    lag_index = jnp.arange(tap_count, dtype=jnp.int32)
    valid_mask = (lag_index[None, :] >= (tap_count - 1 - history_slot)[:, None]).astype(jnp.float32)
    window = window * valid_mask[:, :, None, None]
    weights = conv_taps.astype(jnp.float32)
    conv_sum = (
        jnp.einsum("rkgc,kgc->rgc", window, weights[:tap_count], precision=HIGHEST)
        + weights[tap_count]
    )
    activated = jax.nn.silu(conv_sum)
    inputs = activated[..., :channels].reshape(count_rows, groups, head_count, head_width)
    in_coef = activated[..., channels : channels + state_size]
    out_coef = activated[..., channels + state_size :]
    step_size = jax.nn.softplus(step_raw + step_bias)
    decay_rate = jnp.exp(-step_size * jnp.exp(decay_log))
    updated = (
        decay_rate[..., None, None] * state_groups.astype(jnp.float32)
        + (step_size[..., None] * inputs)[..., None] * in_coef[:, :, None, None, :]
    )
    readout = (
        jnp.einsum("rghpn,rgn->rghp", updated, out_coef, precision=HIGHEST)
        + skip_gain[..., None] * inputs
    )
    gated_out = readout.reshape(count_rows, groups, channels) * jax.nn.silu(inner_terms[:, 0])
    normed = (gated_out * rms_scale(gated_out) * mixer_gain.astype(jnp.float32)).astype(
        jnp.bfloat16
    )
    return (normed, updated.astype(jnp.bfloat16), window[:, 1:].astype(jnp.bfloat16))


def local(
    hidden_in,
    row_owner,
    history_len,
    pre_gain,
    inner_proj,
    select_proj,
    step_proj,
    step_bias,
    decay_log,
    skip_gain,
    conv_taps,
    conv_window,
    state_cache,
    mixer_gain,
    output_proj,
    channel_gain,
    up_weight,
    down_weight,
):
    total_rows, model_width = hidden_in.shape
    head_devices = lax.axis_size(HEAD)
    group_devices = lax.axis_size(GRP)
    own_rows = total_rows // head_devices
    local_groups = conv_taps.shape[1]
    channels = mixer_gain.shape[1]
    state_size = select_proj.shape[2] // local_groups
    per_group = step_proj.shape[1] // local_groups
    head_width = state_cache.shape[2]
    slice_width = model_width // head_devices
    head_index = lax.axis_index(HEAD)
    group_index = lax.axis_index(GRP)
    core = lax.axis_index("c")
    positions = jnp.arange(total_rows, dtype=jnp.int32)
    sort_key = row_owner * total_rows + positions
    slot_of_row = jnp.sum((sort_key[None, :] < sort_key[:, None]).astype(jnp.int32), axis=1)
    to_slot = (slot_of_row[None, :] == positions[:, None]).astype(jnp.bfloat16)
    hidden_wide = hidden_in.astype(jnp.float32)
    scale = rms_scale(hidden_wide)
    base_cols = lax.dynamic_slice_in_dim(
        hidden_in, head_index * slice_width, slice_width, 1
    ).astype(jnp.float32)
    gain_cols = lax.dynamic_slice_in_dim(pre_gain, head_index * slice_width, slice_width, 0)
    local_cols = (base_cols * scale * gain_cols.astype(jnp.float32)).astype(jnp.bfloat16)
    sorted_rows = jnp.dot(to_slot, local_cols)
    inner_flat = inner_proj.reshape(slice_width, -1)
    select_flat = select_proj.reshape(slice_width, -1)
    inner_size = inner_flat.shape[1]
    select_size = select_flat.shape[1]
    terms = jnp.concatenate(
        [
            jnp.dot(sorted_rows, inner_flat, preferred_element_type=jnp.float32),
            jnp.dot(sorted_rows, select_flat, preferred_element_type=jnp.float32),
            jnp.dot(sorted_rows, step_proj, preferred_element_type=jnp.float32),
        ],
        axis=1,
    ).astype(jnp.bfloat16)
    pieces = lax.all_to_all(
        terms.reshape(head_devices, own_rows, -1), HEAD, split_axis=0, concat_axis=0, tiled=True
    )
    projected = jnp.sum(pieces.astype(jnp.float32), axis=0)
    inner_terms = projected[:, :inner_size].reshape(own_rows, 2, local_groups, channels)
    select_terms = projected[:, inner_size : inner_size + select_size].reshape(
        own_rows, 2, local_groups, state_size
    )
    step_raw = projected[:, inner_size + select_size :].reshape(own_rows, local_groups, per_group)
    own_slots = head_index * own_rows + jnp.arange(own_rows, dtype=jnp.int32)
    history_slot = jnp.sum(
        jnp.where(slot_of_row[None, :] == own_slots[:, None], history_len[None, :], 0), axis=1
    )
    state_groups = state_cache.reshape(own_rows, local_groups, per_group, head_width, state_size)
    normed_mix, state_next, window_next = mixer(
        inner_terms,
        select_terms,
        step_raw,
        history_slot,
        step_bias.reshape(local_groups, per_group),
        decay_log.reshape(local_groups, per_group),
        skip_gain.reshape(local_groups, per_group),
        conv_taps,
        conv_window,
        state_groups,
        mixer_gain,
    )
    all_mix = lax.all_to_all(
        jnp.broadcast_to(normed_mix.reshape(1, own_rows, -1), (head_devices, own_rows, channels)),
        HEAD,
        split_axis=0,
        concat_axis=0,
        tiled=True,
    ).reshape(total_rows, channels)
    mixed = jnp.dot(
        all_mix, output_proj.reshape(channels, -1), preferred_element_type=jnp.float32
    ).astype(jnp.bfloat16)
    for axis, bit in (("x", 1), ("x", 3), ("yh", 1)):
        other = swap(mixed, axis, bit)
        mixed = (mixed.astype(jnp.float32) + other.astype(jnp.float32)).astype(jnp.bfloat16)
    mixed_rows = jnp.dot(to_slot.T, mixed, preferred_element_type=jnp.float32)
    hidden_piece = (base_cols + mixed_rows).astype(jnp.bfloat16)
    near = lax.all_to_all(
        jnp.broadcast_to(hidden_piece[None], (head_devices // 2,) + hidden_piece.shape),
        ("z", "yl"),
        split_axis=0,
        concat_axis=0,
        tiled=True,
    )
    far = swap(near, "c", 1)
    even = jnp.where(core == 0, near, far)
    odd = jnp.where(core == 0, far, near)
    residual = jnp.stack([even, odd], axis=1).reshape(head_devices, total_rows, slice_width)
    residual_wide = residual.astype(jnp.float32)
    row_scale = lax.rsqrt(
        jnp.sum(residual_wide * residual_wide, axis=(0, 2)) / model_width + EPS
    )
    ffn_input = (
        residual_wide
        * row_scale[None, :, None]
        * channel_gain.astype(jnp.float32).reshape(head_devices, 1, slice_width)
    ).astype(jnp.bfloat16)
    raised = jnp.maximum(
        jnp.einsum(
            "krd,kdf->rf",
            ffn_input,
            up_weight.reshape(head_devices, slice_width, -1),
            preferred_element_type=jnp.float32,
        ),
        0.0,
    )
    squared = (raised * raised).astype(jnp.bfloat16)
    down_terms = lax.dot_general(
        down_weight, squared, (((0,), (1,)), ((), ())), preferred_element_type=jnp.float32
    ).astype(jnp.bfloat16)
    chips = group_devices * head_devices // 2
    piece_width = model_width // (group_devices * head_devices)
    paired = down_terms.reshape(chips, 2, piece_width, total_rows)
    keep = lax.dynamic_index_in_dim(paired, core, 1, keepdims=False)
    give = lax.dynamic_index_in_dim(paired, 1 - core, 1, keepdims=False)
    chip_sum = (keep.astype(jnp.float32) + swap(give, "c", 1).astype(jnp.float32)).astype(
        jnp.bfloat16
    )
    spread = lax.all_to_all(chip_sum, CHIPS, split_axis=0, concat_axis=0, tiled=True)
    down_total = jnp.sum(spread.astype(jnp.float32), axis=0)
    flat_index = group_index * head_devices + head_index
    per_slice = slice_width // piece_width
    residual_piece = lax.dynamic_slice(
        residual,
        (flat_index // per_slice, 0, (flat_index % per_slice) * piece_width),
        (1, total_rows, piece_width),
    )[0].astype(jnp.float32)
    block_out = (residual_piece.T + down_total).astype(jnp.bfloat16).T
    state_flat = state_next.reshape(own_rows, local_groups * per_group, head_width, state_size)
    return (block_out, state_flat, window_next)


def solution(mesh):
    fine = Mesh(mesh.devices.reshape(4, 2, 4, 2, 2), ("x", "yh", "z", "yl", "c"))
    placed = (
        P(),
        P(),
        P(),
        P(),
        P(HEAD, None, GRP),
        P(HEAD, None, GRP),
        P(HEAD, GRP),
        P(GRP),
        P(GRP),
        P(GRP),
        P(None, GRP, None),
        P(HEAD, None, GRP, None),
        P(HEAD, GRP, None, None),
        P(GRP, None),
        P(GRP, None, HEAD),
        P(),
        P(None, GRP + HEAD),
        P(GRP + HEAD, None),
    )
    return jax.shard_map(
        local,
        mesh=fine,
        in_specs=placed,
        out_specs=(
            P(None, GRP + HEAD),
            P(HEAD, GRP, None, None),
            P(HEAD, None, GRP, None),
        ),
        check_vma=False,
    )
```

```python
import jax
import jax.numpy as jnp
from jax import lax
from jax.experimental import pallas as pl
from jax.experimental.pallas import tpu as pltpu
from jax.sharding import Mesh, PartitionSpec as P

EPS = 1e-05
GRP = ("x", "yh")
HEAD = ("z", "yl", "c")
CHIPS = ("x", "yh", "z", "yl")
NEAR = ("z", "yl")
F32 = jnp.float32
BF16 = jnp.bfloat16
HBM = pl.BlockSpec(memory_space=pltpu.HBM)
ANY = pl.BlockSpec(memory_space=pl.ANY)
VMEM = pl.BlockSpec(memory_space=pltpu.VMEM)
SMEM = pl.BlockSpec(memory_space=pltpu.SMEM)
LANES = 128


def swap(value, axis, bit):
    size = lax.axis_size(axis)
    return lax.ppermute(value, axis, [(i, i ^ bit) for i in range(size)])


def add(left, right):
    return (left.astype(F32) + right.astype(F32)).astype(BF16)


def params(mib):
    return pltpu.CompilerParams(vmem_limit_bytes=mib << 20)


def contract(left, right, left_dim, right_dim):
    return lax.dot_general(
        left, right, (((left_dim,), (right_dim,)), ((), ())), preferred_element_type=F32
    )


def split3(values):
    high = values.astype(BF16)
    rest = values - high.astype(F32)
    middle = rest.astype(BF16)
    low = (rest - middle.astype(F32)).astype(BF16)
    return high, middle, low


def prepare_kernel(
    place,
    hidden,
    owner,
    history,
    gain,
    weights,
    tiles,
    pairs,
    plain,
    order,
    past,
    held,
    gains,
    sems,
    hidden_sems,
):
    head = place[0]
    core = place[1]
    count = tiles.shape[0]
    rows, width = hidden.shape
    part = plain.shape[1]
    blocks = width // part
    own_rows = rows // blocks
    loads = [
        pltpu.make_async_copy(
            hidden.at[:, pl.ds(i * part, part)], held.at[i], hidden_sems.at[i]
        )
        for i in range(blocks)
    ]
    copies = [
        pltpu.make_async_copy(weights.at[:, i], tiles.at[i], sems.at[i]) for i in range(count)
    ]
    for copy in loads + copies:
        copy.start()
    gains[...] = gain[...].astype(F32)
    position = lax.broadcasted_iota(jnp.int32, (rows, rows), 1)
    key = (owner[...] * rows + position).astype(F32)
    before = (key.T < key).astype(F32)
    rank = jnp.sum(before, axis=0, keepdims=True)
    slot = lax.broadcasted_iota(jnp.int32, (rows, rows), 0)
    to_slot = jnp.where(rank == slot.astype(F32), 1.0, 0.0)
    slot_history = jnp.sum(to_slot * history[...].astype(F32), axis=1, keepdims=True)
    past[...] = jnp.broadcast_to(slot_history, (rows, LANES))
    half = rows // 2
    near = slot < half
    inner = jnp.where(near, slot, slot - half)
    shift = jnp.where(near, core, 1 - core) * own_rows
    sent = (inner // own_rows) * (2 * own_rows) + lax.rem(inner, own_rows) + shift
    order[...] = jnp.where(rank == sent.astype(F32), 1.0, 0.0).astype(BF16)
    squares = jnp.zeros((rows, LANES), F32)
    for i in range(blocks):
        loads[i].wait()
        for q in range(part // LANES):
            chunk = held[i, :, q * LANES : (q + 1) * LANES].astype(F32)
            squares += chunk * chunk
    scale = lax.rsqrt(jnp.sum(squares, axis=1, keepdims=True) / width + EPS)
    normed = []
    for q in range(part // LANES):
        chunk = held[head, :, q * LANES : (q + 1) * LANES].astype(F32)
        row = gains[pl.ds(head * (part // LANES) + q, 1), :]
        normed.append((chunk * scale * row).astype(BF16))
    ordered = jnp.dot(
        order[...], jnp.concatenate(normed, axis=1), preferred_element_type=F32
    ).astype(BF16)
    plain[...] = ordered
    source = lax.broadcasted_iota(jnp.int32, (part, 2 * part), 0)
    target = lax.broadcasted_iota(jnp.int32, (part, 2 * part), 1)
    for which in range(2):
        spread = jnp.where(target == 2 * source + which, 1.0, 0.0).astype(BF16)
        pairs[which * rows : (which + 1) * rows, :] = jnp.dot(
            ordered, spread, preferred_element_type=F32
        ).astype(BF16)
    for copy in copies:
        copy.wait()


def project_kernel(pairs, plain, tiles, select, step, keep, give):
    count = tiles.shape[0]
    rows = plain.shape[0]
    half = rows // 2
    left = pairs[...]

    def put(at, values):
        width = values.shape[1]
        for out, part in ((keep, values[:half]), (give, values[half:])):
            out[:, :, at : at + width] = part.reshape(out.shape[0], out.shape[1], width).astype(BF16)

    for i in range(0, count, 2):
        right = jnp.concatenate([tiles[i], tiles[i + 1]], axis=1)
        both = jnp.dot(left, right, preferred_element_type=F32)
        put(i * LANES, both[:rows])
        put((count + i) * LANES, both[rows:])
    both = jnp.dot(left, select[...], preferred_element_type=F32)
    at = 2 * count * LANES
    put(at, both[:rows])
    put(at + LANES, both[rows:])
    steps = contract(plain[...], step[...], 1, 1)
    missing = LANES - steps.shape[1]
    put(at + 2 * LANES, jnp.concatenate([steps, jnp.zeros((rows, missing), F32)], axis=1))


def mixer_kernel(
    place,
    pieces,
    past,
    window,
    taps,
    bias,
    decay_log,
    skip,
    gain,
    state,
    mixed,
    window_next,
    inputs_step,
    in_coef,
    decay,
    held,
    sems,
):
    senders, own, _ = pieces.shape
    channels = mixed.shape[1]
    heads = bias.shape[1]
    width = channels // heads
    copies = [pltpu.make_async_copy(state.at[s], held.at[s], sems.at[s]) for s in range(own)]
    for copy in copies:
        copy.start()
    total = pieces[0].astype(F32)
    for i in range(1, senders):
        total += pieces[i].astype(F32)
    gate = total[:, :channels]
    fresh = total[:, channels : 2 * channels + 2 * LANES].astype(BF16).astype(F32)
    step_raw = total[:, 2 * channels + 2 * LANES : 2 * channels + 2 * LANES + heads]
    valid = past[pl.ds(pl.multiple_of(place[0] * own, own), own), 0:1]
    lags = window.shape[0]
    entries = []
    for k in range(lags):
        mask = jnp.where(valid >= lags - k, 1.0, 0.0)
        entries.append(window[k].astype(F32) * mask)
    entries.append(fresh)
    weights = taps[...].astype(F32)
    conv = weights[lags + 1 : lags + 2]
    for k in range(lags + 1):
        conv = conv + entries[k] * weights[k : k + 1]
    for k in range(lags):
        window_next[k] = entries[k + 1].astype(BF16)
    active = conv * (1.0 / (1.0 + jnp.exp(-conv)))
    u = active[:, :channels]
    b = active[:, channels : channels + LANES]
    c = active[:, channels + LANES :]
    shifted = step_raw + bias[...]
    step = jnp.maximum(shifted, 0.0) + jnp.log1p(jnp.exp(-jnp.abs(shifted)))
    rate = jnp.exp(-step * jnp.exp(decay_log[...]))
    both = jnp.sum(b * c, axis=1, keepdims=True)
    direct = step * both + skip[...]
    head_of = lax.broadcasted_iota(jnp.int32, (heads, channels), 0)
    channel = lax.broadcasted_iota(jnp.int32, (heads, channels), 1)
    first = head_of * width
    spread = jnp.where((channel >= first) & (channel < first + width), 1.0, 0.0).astype(BF16)
    stacked = jnp.concatenate([rate, step, direct], axis=0)
    wide = sum(jnp.dot(part, spread, preferred_element_type=F32) for part in split3(stacked))
    rate_wide = wide[:own]
    step_wide = wide[own : 2 * own]
    direct_wide = wide[2 * own :]
    inputs_step[...] = step_wide * u
    in_coef[...] = b
    decay[...] = rate
    c_high = c.astype(BF16)
    c_low = (c - c_high.astype(F32)).astype(BF16)
    coefs = jnp.concatenate([c_high, c_low], axis=0)
    row = lax.broadcasted_iota(jnp.int32, (own, channels), 0)
    read = jnp.zeros((own, channels), F32)
    for s in range(own):
        copies[s].wait()
        found = contract(coefs, held[s], 1, 1)
        read = jnp.where(row == s, found[:own] + found[own:], read)
    gated = (rate_wide * read + direct_wide * u) * (gate * (1.0 / (1.0 + jnp.exp(-gate))))
    scale = lax.rsqrt(jnp.sum(gated * gated, axis=1, keepdims=True) / channels + EPS)
    mixed[...] = (gated * scale * gain[...].astype(F32)).astype(BF16)


def ffn_kernel(
    place, near, far, gain, up, down, keep, give, slice_out, up_held, down_held, turned, gains, sems
):
    core = place[1]
    flat = place[2]
    chunks, rows, part = near.shape
    hidden = up.shape[2]
    model = 2 * chunks * part
    piece = keep.shape[1]
    ups = [pltpu.make_async_copy(up.at[k], up_held.at[k], sems.at[0, k]) for k in range(2 * chunks)]
    downs = [
        pltpu.make_async_copy(
            down.at[:, pl.ds(k * part, part)], down_held.at[k], sems.at[1, k]
        )
        for k in range(2 * chunks)
    ]
    for copy in ups + downs:
        copy.start()
    gains[...] = gain[...].astype(F32)
    squares = jnp.zeros((rows, LANES), F32)
    total = jnp.zeros((rows, hidden), F32)
    lanes = part // LANES
    for j in range(chunks):
        ups[2 * j].wait()
        ups[2 * j + 1].wait()
        for source, which in ((near, core), (far, 1 - core)):
            scaled = []
            for q in range(lanes):
                chunk = source[j, :, q * LANES : (q + 1) * LANES].astype(F32)
                squares += chunk * chunk
                row = gains[pl.ds((2 * j + which) * lanes + q, 1), :]
                scaled.append((chunk * row).astype(BF16))
            total += jnp.dot(
                jnp.concatenate(scaled, axis=1),
                up_held[2 * j + which],
                preferred_element_type=F32,
            )
    scale = lax.rsqrt(jnp.sum(squares, axis=1, keepdims=True) / model + EPS)
    raised = jnp.maximum(total * scale, 0.0)
    squared = (raised * raised).astype(BF16)
    per_part = part // piece
    owner = flat // per_part
    mine = near[owner // 2].astype(F32)
    other = far[owner // 2].astype(F32)
    turned[...] = jnp.where(lax.rem(owner, 2) == core, mine, other).T
    slice_out[...] = turned[pl.ds(pl.multiple_of(lax.rem(flat, per_part) * piece, piece), piece), :]
    for k in range(2 * chunks):
        downs[k].wait()
        out = jnp.dot(squared, down_held[k], preferred_element_type=F32).astype(BF16).T
        for q in range(part // (2 * piece)):
            low = out[2 * q * piece : (2 * q + 1) * piece]
            high = out[(2 * q + 1) * piece : (2 * q + 2) * piece]
            chip = k * (part // (2 * piece)) + q
            keep[chip] = jnp.where(core == 0, low, high)
            give[chip] = jnp.where(core == 0, high, low)


def local(
    hidden_in,
    row_owner,
    history_len,
    pre_gain,
    inner_proj,
    select_proj,
    step_proj,
    step_bias,
    decay_log,
    skip_gain,
    conv_taps,
    conv_window,
    state_cache,
    mixer_gain,
    output_proj,
    channel_gain,
    up_weight,
    down_weight,
):
    rows, model = hidden_in.shape
    heads_axis = lax.axis_size(HEAD)
    groups_axis = lax.axis_size(GRP)
    own = rows // heads_axis
    part = model // heads_axis
    channels = mixer_gain.shape[1]
    heads = step_proj.shape[1]
    state_size = state_cache.shape[3]
    head_width = state_cache.shape[2]
    taps = conv_taps.shape[0]
    conv_width = conv_taps.shape[2]
    hidden_units = up_weight.shape[1]
    tile_count = channels // LANES
    head_index = lax.axis_index(HEAD)
    group_index = lax.axis_index(GRP)
    core = lax.axis_index("c")
    flat_index = group_index * heads_axis + head_index
    place = jnp.stack([head_index, core, flat_index]).astype(jnp.int32)
    shape = jax.ShapeDtypeStruct

    tiled = inner_proj.reshape(part, 2, tile_count, LANES).transpose(0, 2, 1, 3)
    tiles, pairs, plain, order, past = pl.pallas_call(
        prepare_kernel,
        out_shape=(
            shape((tile_count, part, 2, LANES), BF16),
            shape((2 * rows, 2 * part), BF16),
            shape((rows, part), BF16),
            shape((rows, rows), BF16),
            shape((rows, LANES), F32),
        ),
        in_specs=[SMEM, HBM, VMEM, VMEM, VMEM, HBM],
        out_specs=(ANY, VMEM, VMEM, VMEM, VMEM),
        scratch_shapes=[
            pltpu.VMEM((heads_axis, rows, part), BF16),
            pltpu.VMEM((model // LANES, LANES), F32),
            pltpu.SemaphoreType.DMA((tile_count,)),
            pltpu.SemaphoreType.DMA((heads_axis,)),
        ],
        compiler_params=params(16),
    )(
        place,
        hidden_in,
        row_owner.reshape(1, rows),
        history_len.reshape(1, rows),
        pre_gain.reshape(model // LANES, LANES),
        tiled,
    )
    sent_width = 2 * channels + 2 * state_size + LANES
    near_owners = heads_axis // 2
    keep, give = pl.pallas_call(
        project_kernel,
        out_shape=(shape((near_owners, own, sent_width), BF16),) * 2,
        in_specs=[VMEM] * 5,
        out_specs=(VMEM,) * 2,
        compiler_params=params(16),
    )(
        pairs,
        plain,
        tiles.reshape(tile_count, 2 * part, LANES),
        select_proj.reshape(2 * part, state_size),
        step_proj.T,
    )
    chip_terms = add(keep, swap(give, "c", 1))
    pieces = lax.all_to_all(chip_terms, NEAR, split_axis=0, concat_axis=0, tiled=True)
    mixed_own, window_next, inputs_step, in_coef, decay = pl.pallas_call(
        mixer_kernel,
        out_shape=(
            shape((own, channels), BF16),
            shape((taps - 2, own, conv_width), BF16),
            shape((own, channels), F32),
            shape((own, state_size), F32),
            shape((own, heads), F32),
        ),
        in_specs=[SMEM] + [VMEM] * 8 + [ANY],
        out_specs=(VMEM,) * 5,
        scratch_shapes=[
            pltpu.VMEM((own, heads * head_width, state_size), BF16),
            pltpu.SemaphoreType.DMA((own,)),
        ],
        compiler_params=params(16),
    )(
        place,
        pieces,
        past,
        conv_window.transpose(1, 2, 0, 3).reshape(taps - 2, own, conv_width),
        conv_taps.reshape(taps, conv_width),
        step_bias.reshape(1, heads),
        decay_log.reshape(1, heads),
        skip_gain.reshape(1, heads),
        mixer_gain,
        state_cache.reshape(own, heads * head_width, state_size),
    )
    near_mix = lax.all_to_all(
        jnp.broadcast_to(mixed_own[None], (near_owners, own, channels)),
        NEAR,
        split_axis=0,
        concat_axis=0,
        tiled=True,
    )
    far_mix = swap(near_mix, "c", 1)
    out_weight = output_proj.reshape(channels, part)
    mixed = jnp.concatenate(
        [
            jnp.dot(mix.reshape(rows // 2, channels), out_weight, preferred_element_type=F32)
            for mix in (near_mix, far_mix)
        ]
    ).astype(BF16)
    for axis, bit in (("x", 1), ("x", 3), ("yh", 1)):
        mixed = add(mixed, swap(mixed, axis, bit))
    base_cols = lax.dynamic_slice_in_dim(hidden_in, head_index * part, part, 1).astype(F32)
    mixed_rows = contract(order, mixed, 0, 0)
    hidden_piece = (base_cols + mixed_rows).astype(BF16)
    near = lax.all_to_all(
        jnp.broadcast_to(hidden_piece[None], (heads_axis // 2,) + hidden_piece.shape),
        NEAR,
        split_axis=0,
        concat_axis=0,
        tiled=True,
    )
    far = swap(near, "c", 1)
    chips = groups_axis * heads_axis // 2
    piece = model // (groups_axis * heads_axis)
    keep, give, residual_slice = pl.pallas_call(
        ffn_kernel,
        out_shape=(
            shape((chips, piece, rows), BF16),
            shape((chips, piece, rows), BF16),
            shape((piece, rows), F32),
        ),
        in_specs=[SMEM, VMEM, VMEM, VMEM, HBM, HBM],
        out_specs=(VMEM,) * 3,
        scratch_shapes=[
            pltpu.VMEM((heads_axis, part, hidden_units), BF16),
            pltpu.VMEM((heads_axis, hidden_units, part), BF16),
            pltpu.VMEM((part, rows), F32),
            pltpu.VMEM((model // LANES, LANES), F32),
            pltpu.SemaphoreType.DMA((2, heads_axis)),
        ],
        compiler_params=params(24),
    )(
        place,
        near,
        far,
        channel_gain.reshape(model // LANES, LANES),
        up_weight.reshape(heads_axis, part, hidden_units),
        down_weight,
    )
    chip_sum = add(keep, swap(give, "c", 1))
    spread = lax.all_to_all(chip_sum, CHIPS, split_axis=0, concat_axis=0, tiled=True)
    block_out = (residual_slice + jnp.sum(spread.astype(F32), axis=0)).astype(BF16).T
    step_input = inputs_step.reshape(own, heads, head_width)
    state_next = (
        decay[..., None, None] * state_cache.astype(F32)
        + step_input[..., None] * in_coef[:, None, None, :]
    ).astype(BF16)
    window_out = window_next.reshape(taps - 2, 1, own, conv_width).transpose(2, 0, 1, 3)
    return (block_out, state_next, window_out)


def solution(mesh):
    fine = Mesh(mesh.devices.reshape(4, 2, 4, 2, 2), ("x", "yh", "z", "yl", "c"))
    placed = (
        P(),
        P(),
        P(),
        P(),
        P(HEAD, None, GRP),
        P(HEAD, None, GRP),
        P(HEAD, GRP),
        P(GRP),
        P(GRP),
        P(GRP),
        P(None, GRP, None),
        P(HEAD, None, GRP, None),
        P(HEAD, GRP, None, None),
        P(GRP, None),
        P(GRP, None, HEAD),
        P(),
        P(None, GRP + HEAD),
        P(GRP + HEAD, None),
    )
    return jax.shard_map(
        local,
        mesh=fine,
        in_specs=placed,
        out_specs=(
            P(None, GRP + HEAD),
            P(HEAD, GRP, None, None),
            P(HEAD, None, GRP, None),
        ),
        check_vma=False,
    )
```

```python
import jax
import jax.numpy as jnp
from jax import lax
from jax.experimental import pallas as pl
from jax.experimental.pallas import tpu as pltpu
from jax.sharding import Mesh, PartitionSpec as P

EPS = 1e-05
GRP = ("x", "yh")
HEAD = ("z", "yl", "c")
CHIPS = ("x", "yh", "z", "yl")
NEAR = ("z", "yl")
F32 = jnp.float32
BF16 = jnp.bfloat16
HBM = pl.BlockSpec(memory_space=pltpu.HBM)
ANY = pl.BlockSpec(memory_space=pl.ANY)
VMEM = pl.BlockSpec(memory_space=pltpu.VMEM)
LANES = 128
PREP = 20
FFN = 8
FETCH = 8


def swap(value, axis, bit):
    size = lax.axis_size(axis)
    return lax.ppermute(value, axis, [(i, i ^ bit) for i in range(size)])


def add(left, right):
    return (left.astype(F32) + right.astype(F32)).astype(BF16)


def in_hbm(value):
    return pltpu.with_memory_space_constraint(value, pltpu.HBM)


def params(mib):
    return pltpu.CompilerParams(vmem_limit_bytes=mib << 20)


def contract(left, right, left_dim, right_dim):
    return lax.dot_general(
        left, right, (((left_dim,), (right_dim,)), ((), ())), preferred_element_type=F32
    )


def split3(values):
    high = values.astype(BF16)
    rest = values - high.astype(F32)
    middle = rest.astype(BF16)
    low = (rest - middle.astype(F32)).astype(BF16)
    return high, middle, low


def project_kernel(
    owner,
    history,
    hidden,
    gain,
    weights,
    select,
    step,
    keep,
    give,
    order,
    past,
    base,
    held,
    owner_held,
    history_held,
    gain_held,
    gains,
    tiles,
    select_held,
    step_held,
    sems,
    hidden_sems,
    small_sems,
):
    head = lax.axis_index(HEAD)
    core = lax.axis_index("c")
    count, part = tiles.shape[:2]
    rows, width = hidden.shape
    blocks = width // part
    own_rows = rows // blocks
    half = rows // 2
    smalls = [
        pltpu.make_async_copy(source, target, small_sems.at[i])
        for i, (source, target) in enumerate(
            (
                (owner, owner_held),
                (history, history_held),
                (gain, gain_held),
                (select, select_held),
                (step, step_held),
            )
        )
    ]
    loads = [
        pltpu.make_async_copy(
            hidden.at[:, pl.ds(i * part, part)], held.at[i], hidden_sems.at[i]
        )
        for i in range(blocks)
    ]
    copies = [
        pltpu.make_async_copy(weights.at[:, i], tiles.at[i], sems.at[i]) for i in range(count)
    ]
    for copy in smalls[:3] + loads:
        copy.start()
    later = copies + smalls[3:]
    for copy in smalls[:3]:
        copy.wait()
    gains[...] = gain_held[...].astype(F32)
    position = lax.broadcasted_iota(jnp.int32, (rows, rows), 1)
    key = (owner_held[...] * rows + position).astype(F32)
    before = (key.T < key).astype(F32)
    rank = jnp.sum(before, axis=0, keepdims=True)
    slot = lax.broadcasted_iota(jnp.int32, (rows, rows), 0)
    to_slot = jnp.where(rank == slot.astype(F32), 1.0, 0.0)
    slot_history = jnp.sum(to_slot * history_held[...].astype(F32), axis=1, keepdims=True)
    past[...] = jnp.broadcast_to(slot_history, (rows, LANES))
    near = slot < half
    inner = jnp.where(near, slot, slot - half)
    shift = jnp.where(near, core, 1 - core) * own_rows
    sent = (inner // own_rows) * (2 * own_rows) + lax.rem(inner, own_rows) + shift
    ordering = jnp.where(rank == sent.astype(F32), 1.0, 0.0).astype(BF16)
    order[...] = ordering
    source = lax.broadcasted_iota(jnp.int32, (part, 2 * part), 0)
    target = lax.broadcasted_iota(jnp.int32, (part, 2 * part), 1)
    spread = jnp.where(target == 2 * source, 1.0, 0.0).astype(BF16)
    squares = jnp.zeros((rows, LANES), F32)
    for i in range(blocks):
        loads[i].wait()
        for copy in later[2 * i : 2 * i + 2]:
            copy.start()
        for q in range(part // LANES):
            chunk = held[i, :, q * LANES : (q + 1) * LANES].astype(F32)
            squares += chunk * chunk
    scale = lax.rsqrt(jnp.sum(squares, axis=1, keepdims=True) / width + EPS)
    normed = []
    for q in range(part // LANES):
        chunk = held[head, :, q * LANES : (q + 1) * LANES].astype(F32)
        row = gains[pl.ds(head * (part // LANES) + q, 1), :]
        normed.append((chunk * scale * row).astype(BF16))
    base[...] = held[head]
    plain = jnp.dot(ordering, jnp.concatenate(normed, axis=1), preferred_element_type=F32).astype(
        BF16
    )
    even = jnp.dot(plain, spread, preferred_element_type=F32)
    odd = pltpu.roll(even, 1, axis=1)
    left = jnp.concatenate([even.astype(BF16), odd.astype(BF16)], axis=0)

    def put(at, values):
        width = values.shape[1]
        for out, part in ((keep, values[:half]), (give, values[half:])):
            out[:, at : at + width] = part.astype(BF16)

    for i in range(0, count, 2):
        copies[i].wait()
        copies[i + 1].wait()
        right = jnp.concatenate(
            [tiles.at[i + k].reshape(2 * part, LANES)[...] for k in range(2)], axis=1
        )
        both = jnp.dot(left, right, preferred_element_type=F32)
        put(i * LANES, both[:rows])
        put((count + i) * LANES, both[rows:])
    for copy in smalls[3:]:
        copy.wait()
    both = jnp.dot(left, select_held[...], preferred_element_type=F32)
    at = 2 * count * LANES
    put(at, both[:rows])
    put(at + LANES, both[rows:])
    steps = contract(plain, step_held[...], 1, 1)
    missing = LANES - steps.shape[1]
    put(at + 2 * LANES, jnp.concatenate([steps, jnp.zeros((rows, missing), F32)], axis=1))


def mixer_kernel(
    pieces,
    past,
    window,
    taps,
    bias,
    decay_log,
    skip,
    gain,
    state,
    mixed,
    window_next,
    inputs_step,
    in_coef,
    decay,
):
    senders, own, _ = pieces.shape
    channels = mixed.shape[1]
    heads = bias.shape[1]
    width = channels // heads
    total = pieces[0].astype(F32)
    for i in range(1, senders):
        total += pieces[i].astype(F32)
    gate = total[:, :channels]
    fresh = total[:, channels : 2 * channels + 2 * LANES].astype(BF16).astype(F32)
    step_raw = total[:, 2 * channels + 2 * LANES : 2 * channels + 2 * LANES + heads]
    valid = past[pl.ds(pl.multiple_of(lax.axis_index(HEAD) * own, own), own), 0:1]
    lags = window.shape[0]
    entries = []
    for k in range(lags):
        mask = jnp.where(valid >= lags - k, 1.0, 0.0)
        entries.append(window[k].astype(F32) * mask)
    entries.append(fresh)
    weights = taps[...].astype(F32)
    conv = weights[lags + 1 : lags + 2]
    for k in range(lags + 1):
        conv = conv + entries[k] * weights[k : k + 1]
    for k in range(lags):
        window_next[k] = entries[k + 1].astype(BF16)
    active = conv * (1.0 / (1.0 + jnp.exp(-conv)))
    u = active[:, :channels]
    b = active[:, channels : channels + LANES]
    c = active[:, channels + LANES :]
    shifted = step_raw + bias[...]
    step = jnp.maximum(shifted, 0.0) + jnp.log1p(jnp.exp(-jnp.abs(shifted)))
    rate = jnp.exp(-step * jnp.exp(decay_log[...]))
    both = jnp.sum(b * c, axis=1, keepdims=True)
    direct = step * both + skip[...]
    head_of = lax.broadcasted_iota(jnp.int32, (heads, channels), 0)
    channel = lax.broadcasted_iota(jnp.int32, (heads, channels), 1)
    first = head_of * width
    spread = jnp.where((channel >= first) & (channel < first + width), 1.0, 0.0).astype(BF16)
    stacked = jnp.concatenate([rate, step, direct], axis=0)
    wide = sum(jnp.dot(part, spread, preferred_element_type=F32) for part in split3(stacked))
    rate_wide = wide[:own]
    step_wide = wide[own : 2 * own]
    direct_wide = wide[2 * own :]
    inputs_step[...] = step_wide * u
    in_coef[...] = b
    decay[...] = rate
    c_high = c.astype(BF16)
    c_low = (c - c_high.astype(F32)).astype(BF16)
    coefs = jnp.concatenate([c_high, c_low], axis=0)
    row = lax.broadcasted_iota(jnp.int32, (own, channels), 0)
    read = jnp.zeros((own, channels), F32)
    for s in range(own):
        found = contract(coefs, state[s], 1, 1)
        read = jnp.where(row == s, found[:own] + found[own:], read)
    gated = (rate_wide * read + direct_wide * u) * (gate * (1.0 / (1.0 + jnp.exp(-gate))))
    scale = lax.rsqrt(jnp.sum(gated * gated, axis=1, keepdims=True) / channels + EPS)
    mixed[...] = (gated * scale * gain[...].astype(F32)).astype(BF16)


def add_kernel(left, right, out):
    for i in range(out.shape[0]):
        out[i] = (left[i].astype(F32) + right[i].astype(F32)).astype(BF16)


def residual_kernel(mixed, other, order, base, out):
    total = (mixed[...].astype(F32) + other[...].astype(F32)).astype(BF16)
    piece = (base[...].astype(F32) + contract(order[...], total, 0, 0)).astype(BF16)
    for i in range(out.shape[0]):
        out[i] = piece


def fetch_kernel(after, source, out, sem):
    copy = pltpu.make_async_copy(source, out, sem)
    copy.start()
    copy.wait()


def fetch(after, source):
    return pl.pallas_call(
        fetch_kernel,
        out_shape=pltpu.VMEM(source.shape, source.dtype),
        in_specs=[ANY, HBM],
        out_specs=VMEM,
        scratch_shapes=[pltpu.SemaphoreType.DMA],
        compiler_params=params(FETCH),
        cost_estimate=pl.CostEstimate(
            flops=0, bytes_accessed=2 * source.size * source.dtype.itemsize, transcendentals=0
        ),
    )(after, in_hbm(source))


def ffn_kernel(
    near,
    far,
    gain,
    up,
    down,
    keep,
    give,
    slice_out,
    turned,
    gains,
):
    core = lax.axis_index("c")
    flat = lax.axis_index(GRP + HEAD)
    chunks, rows, part = near.shape
    hidden = up.shape[2]
    model = 2 * chunks * part
    piece = keep.shape[1]
    turns = [(j, which) for which in range(2) for j in range(chunks)]
    gains[...] = gain[...].astype(F32)
    squares = jnp.zeros((rows, LANES), F32)
    total = jnp.zeros((rows, hidden), F32)
    lanes = part // LANES
    for k, (j, which) in enumerate(turns):
        source = near if which == 0 else far
        at = 2 * j + (core if which == 0 else 1 - core)
        scaled = []
        for q in range(lanes):
            chunk = source[j, :, q * LANES : (q + 1) * LANES].astype(F32)
            squares += chunk * chunk
            row = gains[pl.ds(at * lanes + q, 1), :]
            scaled.append((chunk * row).astype(BF16))
        total += jnp.dot(jnp.concatenate(scaled, axis=1), up[at], preferred_element_type=F32)
    scale = lax.rsqrt(jnp.sum(squares, axis=1, keepdims=True) / model + EPS)
    raised = jnp.maximum(total * scale, 0.0)
    squared = (raised * raised).astype(BF16)
    per_part = part // piece
    owner = flat // per_part
    mine = near[owner // 2].astype(F32)
    other = far[owner // 2].astype(F32)
    turned[...] = jnp.where(lax.rem(owner, 2) == core, mine, other).T
    slice_out[...] = turned[pl.ds(pl.multiple_of(lax.rem(flat, per_part) * piece, piece), piece), :]
    for k in range(2 * chunks):
        right = down[:, k * part : (k + 1) * part]
        out = jnp.dot(squared, right, preferred_element_type=F32).astype(BF16).T
        for q in range(part // (2 * piece)):
            low = out[2 * q * piece : (2 * q + 1) * piece]
            high = out[(2 * q + 1) * piece : (2 * q + 2) * piece]
            chip = k * (part // (2 * piece)) + q
            keep[chip] = jnp.where(core == 0, low, high)
            give[chip] = jnp.where(core == 0, high, low)


def local(
    hidden_in,
    row_owner,
    history_len,
    pre_gain,
    inner_proj,
    select_proj,
    step_proj,
    step_bias,
    decay_log,
    skip_gain,
    conv_taps,
    conv_window,
    state_cache,
    mixer_gain,
    output_proj,
    channel_gain,
    up_weight,
    down_weight,
):
    rows, model = hidden_in.shape
    heads_axis = lax.axis_size(HEAD)
    groups_axis = lax.axis_size(GRP)
    own = rows // heads_axis
    part = model // heads_axis
    channels = mixer_gain.shape[1]
    heads = step_proj.shape[1]
    state_size = state_cache.shape[3]
    head_width = state_cache.shape[2]
    taps = conv_taps.shape[0]
    conv_width = conv_taps.shape[2]
    hidden_units = up_weight.shape[1]
    tile_count = channels // LANES
    head_index = lax.axis_index(HEAD)
    shape = jax.ShapeDtypeStruct

    tiled = inner_proj.reshape(part, 2, tile_count, LANES).transpose(0, 2, 1, 3)
    sent_width = 2 * channels + 2 * state_size + LANES
    near_owners = heads_axis // 2
    keep, give, order, past, base = pl.pallas_call(
        project_kernel,
        out_shape=(
            pltpu.VMEM((rows // 2, sent_width), BF16),
            pltpu.VMEM((rows // 2, sent_width), BF16),
            shape((rows, rows), BF16),
            pltpu.VMEM((rows, LANES), F32),
            shape((rows, part), BF16),
        ),
        in_specs=[HBM] * 7,
        out_specs=(VMEM,) * 5,
        scratch_shapes=[
            pltpu.VMEM((heads_axis, rows, part), BF16),
            pltpu.VMEM((1, rows), jnp.int32),
            pltpu.VMEM((1, rows), jnp.int32),
            pltpu.VMEM((model // LANES, LANES), BF16),
            pltpu.VMEM((model // LANES, LANES), F32),
            pltpu.VMEM((tile_count, part, 2, LANES), BF16),
            pltpu.VMEM((2 * part, state_size), BF16),
            pltpu.VMEM((heads, part), BF16),
            pltpu.SemaphoreType.DMA((tile_count,)),
            pltpu.SemaphoreType.DMA((heads_axis,)),
            pltpu.SemaphoreType.DMA((5,)),
        ],
        compiler_params=params(PREP),
    )(
        *(
            in_hbm(value)
            for value in (
                row_owner.reshape(1, rows),
                history_len.reshape(1, rows),
                hidden_in,
                pre_gain.reshape(model // LANES, LANES),
                tiled,
                select_proj.reshape(2 * part, state_size),
                step_proj.T,
            )
        )
    )
    keep, give = (value.reshape(near_owners, own, sent_width) for value in (keep, give))
    chip_terms = add(keep, swap(give, "c", 1))
    pieces = lax.all_to_all(chip_terms, NEAR, split_axis=0, concat_axis=0, tiled=True)
    mixed_own, window_next, inputs_step, in_coef, decay = pl.pallas_call(
        mixer_kernel,
        out_shape=(
            shape((own, channels), BF16),
            shape((taps - 2, own, conv_width), BF16),
            shape((own, channels), F32),
            shape((own, state_size), F32),
            shape((own, heads), F32),
        ),
        in_specs=[VMEM] * 9,
        out_specs=(VMEM,) * 5,
        compiler_params=params(16),
    )(
        pieces,
        past,
        conv_window.transpose(1, 2, 0, 3).reshape(taps - 2, own, conv_width),
        conv_taps.reshape(taps, conv_width),
        step_bias.reshape(1, heads),
        decay_log.reshape(1, heads),
        skip_gain.reshape(1, heads),
        mixer_gain,
        state_cache.reshape(own, heads * head_width, state_size),
    )
    near_mix = lax.all_to_all(
        jnp.broadcast_to(mixed_own[None], (near_owners, own, channels)),
        NEAR,
        split_axis=0,
        concat_axis=0,
        tiled=True,
    )
    far_mix = swap(near_mix, "c", 1)
    out_weight = output_proj.reshape(channels, part)
    mixed = jnp.concatenate(
        [
            jnp.dot(mix.reshape(rows // 2, channels), out_weight, preferred_element_type=F32)
            for mix in (near_mix, far_mix)
        ]
    ).astype(BF16)
    for bit in (1, 3):
        mixed = add(mixed, swap(mixed, "x", bit))
    other = swap(mixed, "yh", 1)
    down_near = fetch(mixed, down_weight)
    other, down_near = lax.optimization_barrier((other, down_near))
    spread_piece = pl.pallas_call(
        residual_kernel,
        out_shape=shape((near_owners, rows, part), BF16),
        in_specs=[VMEM] * 4,
        out_specs=VMEM,
        compiler_params=params(4),
    )(mixed, other, order, base)
    near = lax.all_to_all(spread_piece, NEAR, split_axis=0, concat_axis=0, tiled=True)
    far = swap(near, "c", 1)
    up_near = fetch(near, up_weight.reshape(heads_axis, part, hidden_units))
    far, up_near = lax.optimization_barrier((far, up_near))
    chips = groups_axis * heads_axis // 2
    piece = model // (groups_axis * heads_axis)
    keep, give, residual_slice = pl.pallas_call(
        ffn_kernel,
        out_shape=(
            shape((chips, piece, rows), BF16),
            shape((chips, piece, rows), BF16),
            shape((piece, rows), F32),
        ),
        in_specs=[VMEM] * 5,
        out_specs=(VMEM,) * 3,
        scratch_shapes=[
            pltpu.VMEM((part, rows), F32),
            pltpu.VMEM((model // LANES, LANES), F32),
        ],
        compiler_params=params(FFN),
    )(
        near,
        far,
        channel_gain.reshape(model // LANES, LANES),
        up_near,
        down_near,
    )
    chip_sum = pl.pallas_call(
        add_kernel,
        out_shape=pltpu.VMEM(keep.shape, BF16),
        in_specs=[VMEM] * 2,
        out_specs=VMEM,
        compiler_params=params(4),
    )(keep, swap(give, "c", 1))
    spread = lax.all_to_all(chip_sum, CHIPS, split_axis=0, concat_axis=0, tiled=True)
    block_out = (residual_slice + jnp.sum(spread.astype(F32), axis=0)).astype(BF16).T
    step_input = inputs_step.reshape(own, heads, head_width)
    state_next = (
        decay[..., None, None] * state_cache.astype(F32)
        + step_input[..., None] * in_coef[:, None, None, :]
    ).astype(BF16)
    window_out = window_next.reshape(taps - 2, 1, own, conv_width).transpose(2, 0, 1, 3)
    return (block_out, state_next, window_out)


def solution(mesh):
    fine = Mesh(mesh.devices.reshape(4, 2, 4, 2, 2), ("x", "yh", "z", "yl", "c"))
    placed = (
        P(),
        P(),
        P(),
        P(),
        P(HEAD, None, GRP),
        P(HEAD, None, GRP),
        P(HEAD, GRP),
        P(GRP),
        P(GRP),
        P(GRP),
        P(None, GRP, None),
        P(HEAD, None, GRP, None),
        P(HEAD, GRP, None, None),
        P(GRP, None),
        P(GRP, None, HEAD),
        P(),
        P(None, GRP + HEAD),
        P(GRP + HEAD, None),
    )
    return jax.shard_map(
        local,
        mesh=fine,
        in_specs=placed,
        out_specs=(
            P(None, GRP + HEAD),
            P(HEAD, GRP, None, None),
            P(HEAD, None, GRP, None),
        ),
        check_vma=False,
    )
```

```python
import jax
import jax.numpy as jnp
from jax import lax
from jax.experimental import pallas as pl
from jax.experimental.pallas import tpu as pltpu
from jax.sharding import Mesh, PartitionSpec as P

EPS = 1e-05
GRP = ("x", "yh")
HEAD = ("z", "yl", "c")
CHIPS = ("x", "yh", "z", "yl")
NEAR = ("z", "yl")
F32 = jnp.float32
BF16 = jnp.bfloat16
HBM = pl.BlockSpec(memory_space=pltpu.HBM)
ANY = pl.BlockSpec(memory_space=pl.ANY)
VMEM = pl.BlockSpec(memory_space=pltpu.VMEM)
LANES = 128
PREP = 20
FFN = 8
FETCH = 8


def swap(value, axis, bit):
    size = lax.axis_size(axis)
    return lax.ppermute(value, axis, [(i, i ^ bit) for i in range(size)])


def add(left, right):
    return (left.astype(F32) + right.astype(F32)).astype(BF16)


def in_hbm(value):
    return pltpu.with_memory_space_constraint(value, pltpu.HBM)


def params(mib):
    return pltpu.CompilerParams(vmem_limit_bytes=mib << 20)


def contract(left, right, left_dim, right_dim):
    return lax.dot_general(
        left, right, (((left_dim,), (right_dim,)), ((), ())), preferred_element_type=F32
    )


def split3(values):
    high = values.astype(BF16)
    rest = values - high.astype(F32)
    middle = rest.astype(BF16)
    low = (rest - middle.astype(F32)).astype(BF16)
    return high, middle, low


def project_kernel(
    owner,
    history,
    hidden,
    gain,
    weights,
    select,
    step,
    keep,
    give,
    order,
    past,
    base,
    held,
    owner_held,
    history_held,
    gain_held,
    gains,
    tiles,
    select_held,
    step_held,
    sems,
    hidden_sems,
    small_sems,
):
    head = lax.axis_index(HEAD)
    core = lax.axis_index("c")
    count, part = tiles.shape[:2]
    rows, width = hidden.shape
    blocks = width // part
    own_rows = rows // blocks
    half = rows // 2
    smalls = [
        pltpu.make_async_copy(source, target, small_sems.at[i])
        for i, (source, target) in enumerate(
            (
                (owner, owner_held),
                (history, history_held),
                (gain, gain_held),
                (select, select_held),
                (step, step_held),
            )
        )
    ]
    loads = [
        pltpu.make_async_copy(
            hidden.at[:, pl.ds(i * part, part)], held.at[i], hidden_sems.at[i]
        )
        for i in range(blocks)
    ]
    copies = [
        pltpu.make_async_copy(weights.at[:, i], tiles.at[i], sems.at[i]) for i in range(count)
    ]
    for copy in smalls[:3] + loads:
        copy.start()
    later = copies + smalls[3:]
    for copy in smalls[:3]:
        copy.wait()
    gains[...] = gain_held[...].astype(F32)
    position = lax.broadcasted_iota(jnp.int32, (rows, rows), 1)
    key = (owner_held[...] * rows + position).astype(F32)
    before = (key.T < key).astype(F32)
    rank = jnp.sum(before, axis=0, keepdims=True)
    slot = lax.broadcasted_iota(jnp.int32, (rows, rows), 0)
    to_slot = jnp.where(rank == slot.astype(F32), 1.0, 0.0)
    slot_history = jnp.sum(to_slot * history_held[...].astype(F32), axis=1, keepdims=True)
    past[...] = jnp.broadcast_to(slot_history, (rows, LANES))
    near = slot < half
    inner = jnp.where(near, slot, slot - half)
    shift = jnp.where(near, core, 1 - core) * own_rows
    sent = (inner // own_rows) * (2 * own_rows) + lax.rem(inner, own_rows) + shift
    ordering = jnp.where(rank == sent.astype(F32), 1.0, 0.0).astype(BF16)
    order[...] = ordering
    source = lax.broadcasted_iota(jnp.int32, (part, 2 * part), 0)
    target = lax.broadcasted_iota(jnp.int32, (part, 2 * part), 1)
    spread = jnp.where(target == 2 * source, 1.0, 0.0).astype(BF16)
    squares = jnp.zeros((rows, LANES), F32)
    for i in range(blocks):
        loads[i].wait()
        for copy in later[2 * i : 2 * i + 2]:
            copy.start()
        for q in range(part // LANES):
            chunk = held[i, :, q * LANES : (q + 1) * LANES].astype(F32)
            squares += chunk * chunk
    scale = lax.rsqrt(jnp.sum(squares, axis=1, keepdims=True) / width + EPS)
    normed = []
    for q in range(part // LANES):
        chunk = held[head, :, q * LANES : (q + 1) * LANES].astype(F32)
        row = gains[pl.ds(head * (part // LANES) + q, 1), :]
        normed.append((chunk * scale * row).astype(BF16))
    base[...] = held[head]
    plain = jnp.dot(ordering, jnp.concatenate(normed, axis=1), preferred_element_type=F32).astype(
        BF16
    )
    even = jnp.dot(plain, spread, preferred_element_type=F32)
    odd = pltpu.roll(even, 1, axis=1)
    left = jnp.concatenate([even.astype(BF16), odd.astype(BF16)], axis=0)

    def put(at, values):
        width = values.shape[1]
        for out, part in ((keep, values[:half]), (give, values[half:])):
            out[:, at : at + width] = part.astype(BF16)

    for i in range(0, count, 2):
        copies[i].wait()
        copies[i + 1].wait()
        right = jnp.concatenate(
            [tiles.at[i + k].reshape(2 * part, LANES)[...] for k in range(2)], axis=1
        )
        both = jnp.dot(left, right, preferred_element_type=F32)
        put(i * LANES, both[:rows])
        put((count + i) * LANES, both[rows:])
    for copy in smalls[3:]:
        copy.wait()
    both = jnp.dot(left, select_held[...], preferred_element_type=F32)
    at = 2 * count * LANES
    put(at, both[:rows])
    put(at + LANES, both[rows:])
    steps = contract(plain, step_held[...], 1, 1)
    missing = LANES - steps.shape[1]
    put(at + 2 * LANES, jnp.concatenate([steps, jnp.zeros((rows, missing), F32)], axis=1))


def mixer_kernel(
    pieces,
    past,
    window,
    taps,
    bias,
    decay_log,
    skip,
    gain,
    state,
    mixed,
    window_next,
    inputs_step,
    in_coef,
    decay,
):
    senders, own, _ = pieces.shape
    channels = mixed.shape[1]
    heads = bias.shape[1]
    width = channels // heads
    total = pieces[0].astype(F32)
    for i in range(1, senders):
        total += pieces[i].astype(F32)
    gate = total[:, :channels]
    fresh = total[:, channels : 2 * channels + 2 * LANES].astype(BF16).astype(F32)
    step_raw = total[:, 2 * channels + 2 * LANES : 2 * channels + 2 * LANES + heads]
    valid = past[pl.ds(pl.multiple_of(lax.axis_index(HEAD) * own, own), own), 0:1]
    lags = window.shape[0]
    entries = []
    for k in range(lags):
        mask = jnp.where(valid >= lags - k, 1.0, 0.0)
        entries.append(window[k].astype(F32) * mask)
    entries.append(fresh)
    weights = taps[...].astype(F32)
    conv = weights[lags + 1 : lags + 2]
    for k in range(lags + 1):
        conv = conv + entries[k] * weights[k : k + 1]
    for k in range(lags):
        window_next[k] = entries[k + 1].astype(BF16)
    active = conv * (1.0 / (1.0 + jnp.exp(-conv)))
    u = active[:, :channels]
    b = active[:, channels : channels + LANES]
    c = active[:, channels + LANES :]
    shifted = step_raw + bias[...]
    step = jnp.maximum(shifted, 0.0) + jnp.log1p(jnp.exp(-jnp.abs(shifted)))
    rate = jnp.exp(-step * jnp.exp(decay_log[...]))
    both = jnp.sum(b * c, axis=1, keepdims=True)
    direct = step * both + skip[...]
    head_of = lax.broadcasted_iota(jnp.int32, (heads, channels), 0)
    channel = lax.broadcasted_iota(jnp.int32, (heads, channels), 1)
    first = head_of * width
    spread = jnp.where((channel >= first) & (channel < first + width), 1.0, 0.0).astype(BF16)
    stacked = jnp.concatenate([rate, step, direct], axis=0)
    wide = sum(jnp.dot(part, spread, preferred_element_type=F32) for part in split3(stacked))
    rate_wide = wide[:own]
    step_wide = wide[own : 2 * own]
    direct_wide = wide[2 * own :]
    inputs_step[...] = step_wide * u
    in_coef[...] = b
    decay[...] = rate
    c_high = c.astype(BF16)
    c_low = (c - c_high.astype(F32)).astype(BF16)
    coefs = jnp.concatenate([c_high, c_low], axis=0)
    row = lax.broadcasted_iota(jnp.int32, (own, channels), 0)
    read = jnp.zeros((own, channels), F32)
    for s in range(own):
        found = contract(coefs, state[s], 1, 1)
        read = jnp.where(row == s, found[:own] + found[own:], read)
    gated = (rate_wide * read + direct_wide * u) * (gate * (1.0 / (1.0 + jnp.exp(-gate))))
    scale = lax.rsqrt(jnp.sum(gated * gated, axis=1, keepdims=True) / channels + EPS)
    mixed[...] = (gated * scale * gain[...].astype(F32)).astype(BF16)


def add_kernel(left, right, out):
    for i in range(out.shape[0]):
        out[i] = (left[i].astype(F32) + right[i].astype(F32)).astype(BF16)


def residual_kernel(mixed, other, order, base, out):
    total = (mixed[...].astype(F32) + other[...].astype(F32)).astype(BF16)
    piece = (base[...].astype(F32) + contract(order[...], total, 0, 0)).astype(BF16)
    for i in range(out.shape[0]):
        out[i] = piece


def fetch_kernel(after, source, out, sem):
    copy = pltpu.make_async_copy(source, out, sem)
    copy.start()
    copy.wait()


def fetch(after, source):
    return pl.pallas_call(
        fetch_kernel,
        out_shape=pltpu.VMEM(source.shape, source.dtype),
        in_specs=[ANY, HBM],
        out_specs=VMEM,
        scratch_shapes=[pltpu.SemaphoreType.DMA],
        compiler_params=params(FETCH),
        cost_estimate=pl.CostEstimate(
            flops=0, bytes_accessed=2 * source.size * source.dtype.itemsize, transcendentals=0
        ),
    )(after, in_hbm(source))


def ffn_kernel(
    near,
    far,
    gain,
    up,
    down,
    keep,
    give,
    slice_out,
    turned,
    gains,
):
    core = lax.axis_index("c")
    flat = lax.axis_index(GRP + HEAD)
    chunks, rows, part = near.shape
    hidden = up.shape[2]
    model = 2 * chunks * part
    piece = keep.shape[1]
    turns = [(j, which) for which in range(2) for j in range(chunks)]
    gains[...] = gain[...].astype(F32)
    squares = jnp.zeros((rows, LANES), F32)
    total = jnp.zeros((rows, hidden), F32)
    lanes = part // LANES
    for k, (j, which) in enumerate(turns):
        source = near if which == 0 else far
        at = 2 * j + (core if which == 0 else 1 - core)
        scaled = []
        for q in range(lanes):
            chunk = source[j, :, q * LANES : (q + 1) * LANES].astype(F32)
            squares += chunk * chunk
            row = gains[pl.ds(at * lanes + q, 1), :]
            scaled.append((chunk * row).astype(BF16))
        total += jnp.dot(jnp.concatenate(scaled, axis=1), up[at], preferred_element_type=F32)
    scale = lax.rsqrt(jnp.sum(squares, axis=1, keepdims=True) / model + EPS)
    raised = jnp.maximum(total * scale, 0.0)
    squared = (raised * raised).astype(BF16)
    per_part = part // piece
    owner = flat // per_part
    mine = near[owner // 2].astype(F32)
    other = far[owner // 2].astype(F32)
    turned[...] = jnp.where(lax.rem(owner, 2) == core, mine, other).T
    slice_out[...] = turned[pl.ds(pl.multiple_of(lax.rem(flat, per_part) * piece, piece), piece), :]
    for k in range(2 * chunks):
        right = down[:, k * part : (k + 1) * part]
        out = jnp.dot(squared, right, preferred_element_type=F32).astype(BF16).T
        for q in range(part // (2 * piece)):
            low = out[2 * q * piece : (2 * q + 1) * piece]
            high = out[(2 * q + 1) * piece : (2 * q + 2) * piece]
            chip = k * (part // (2 * piece)) + q
            keep[chip] = jnp.where(core == 0, low, high)
            give[chip] = jnp.where(core == 0, high, low)


def local(
    hidden_in,
    row_owner,
    history_len,
    pre_gain,
    inner_proj,
    select_proj,
    step_proj,
    step_bias,
    decay_log,
    skip_gain,
    conv_taps,
    conv_window,
    state_cache,
    mixer_gain,
    output_proj,
    channel_gain,
    up_weight,
    down_weight,
):
    rows, model = hidden_in.shape
    heads_axis = lax.axis_size(HEAD)
    groups_axis = lax.axis_size(GRP)
    own = rows // heads_axis
    part = model // heads_axis
    channels = mixer_gain.shape[1]
    heads = step_proj.shape[1]
    state_size = state_cache.shape[3]
    head_width = state_cache.shape[2]
    taps = conv_taps.shape[0]
    conv_width = conv_taps.shape[2]
    hidden_units = up_weight.shape[1]
    tile_count = channels // LANES
    head_index = lax.axis_index(HEAD)
    shape = jax.ShapeDtypeStruct

    tiled = inner_proj.reshape(part, 2, tile_count, LANES).transpose(0, 2, 1, 3)
    sent_width = 2 * channels + 2 * state_size + LANES
    near_owners = heads_axis // 2
    keep, give, order, past, base = pl.pallas_call(
        project_kernel,
        out_shape=(
            pltpu.VMEM((rows // 2, sent_width), BF16),
            pltpu.VMEM((rows // 2, sent_width), BF16),
            shape((rows, rows), BF16),
            pltpu.VMEM((rows, LANES), F32),
            shape((rows, part), BF16),
        ),
        in_specs=[HBM] * 7,
        out_specs=(VMEM,) * 5,
        scratch_shapes=[
            pltpu.VMEM((heads_axis, rows, part), BF16),
            pltpu.VMEM((1, rows), jnp.int32),
            pltpu.VMEM((1, rows), jnp.int32),
            pltpu.VMEM((model // LANES, LANES), BF16),
            pltpu.VMEM((model // LANES, LANES), F32),
            pltpu.VMEM((tile_count, part, 2, LANES), BF16),
            pltpu.VMEM((2 * part, state_size), BF16),
            pltpu.VMEM((heads, part), BF16),
            pltpu.SemaphoreType.DMA((tile_count,)),
            pltpu.SemaphoreType.DMA((heads_axis,)),
            pltpu.SemaphoreType.DMA((5,)),
        ],
        compiler_params=params(PREP),
    )(
        *(
            in_hbm(value)
            for value in (
                row_owner.reshape(1, rows),
                history_len.reshape(1, rows),
                hidden_in,
                pre_gain.reshape(model // LANES, LANES),
                tiled,
                select_proj.reshape(2 * part, state_size),
                step_proj.T,
            )
        )
    )
    keep, give = (value.reshape(near_owners, own, sent_width) for value in (keep, give))
    chip_terms = add(keep, swap(give, "c", 1))
    pieces = lax.all_to_all(chip_terms, NEAR, split_axis=0, concat_axis=0, tiled=True)
    mixed_own, window_next, inputs_step, in_coef, decay = pl.pallas_call(
        mixer_kernel,
        out_shape=(
            shape((own, channels), BF16),
            shape((taps - 2, own, conv_width), BF16),
            shape((own, channels), F32),
            shape((own, state_size), F32),
            shape((own, heads), F32),
        ),
        in_specs=[VMEM] * 9,
        out_specs=(VMEM,) * 5,
        compiler_params=params(16),
    )(
        pieces,
        past,
        conv_window.transpose(1, 2, 0, 3).reshape(taps - 2, own, conv_width),
        conv_taps.reshape(taps, conv_width),
        step_bias.reshape(1, heads),
        decay_log.reshape(1, heads),
        skip_gain.reshape(1, heads),
        mixer_gain,
        state_cache.reshape(own, heads * head_width, state_size),
    )
    near_mix = lax.all_to_all(
        jnp.broadcast_to(mixed_own[None], (near_owners, own, channels)),
        NEAR,
        split_axis=0,
        concat_axis=0,
        tiled=True,
    )
    near_mix, inputs_step, in_coef, decay = lax.optimization_barrier(
        (near_mix, inputs_step, in_coef, decay)
    )
    far_mix = swap(near_mix, "c", 1)
    out_weight = output_proj.reshape(channels, part)
    mixed = jnp.concatenate(
        [
            jnp.dot(mix.reshape(rows // 2, channels), out_weight, preferred_element_type=F32)
            for mix in (near_mix, far_mix)
        ]
    ).astype(BF16)
    step_input = inputs_step.reshape(own, heads, head_width)
    state_next = (
        decay[..., None, None] * state_cache.astype(F32)
        + step_input[..., None] * in_coef[:, None, None, :]
    ).astype(BF16)
    for bit in (1, 3):
        other = swap(mixed, "x", bit)
        if bit == 1:
            other, state_next = lax.optimization_barrier((other, state_next))
        mixed = add(mixed, other)
    other = swap(mixed, "yh", 1)
    down_near = fetch(mixed, down_weight)
    other, down_near = lax.optimization_barrier((other, down_near))
    spread_piece = pl.pallas_call(
        residual_kernel,
        out_shape=shape((near_owners, rows, part), BF16),
        in_specs=[VMEM] * 4,
        out_specs=VMEM,
        compiler_params=params(4),
    )(mixed, other, order, base)
    near = lax.all_to_all(spread_piece, NEAR, split_axis=0, concat_axis=0, tiled=True)
    far = swap(near, "c", 1)
    up_near = fetch(near, up_weight.reshape(heads_axis, part, hidden_units))
    far, up_near = lax.optimization_barrier((far, up_near))
    chips = groups_axis * heads_axis // 2
    piece = model // (groups_axis * heads_axis)
    keep, give, residual_slice = pl.pallas_call(
        ffn_kernel,
        out_shape=(
            shape((chips, piece, rows), BF16),
            shape((chips, piece, rows), BF16),
            shape((piece, rows), F32),
        ),
        in_specs=[VMEM] * 5,
        out_specs=(VMEM,) * 3,
        scratch_shapes=[
            pltpu.VMEM((part, rows), F32),
            pltpu.VMEM((model // LANES, LANES), F32),
        ],
        compiler_params=params(FFN),
    )(
        near,
        far,
        channel_gain.reshape(model // LANES, LANES),
        up_near,
        down_near,
    )
    chip_sum = pl.pallas_call(
        add_kernel,
        out_shape=pltpu.VMEM(keep.shape, BF16),
        in_specs=[VMEM] * 2,
        out_specs=VMEM,
        compiler_params=params(4),
    )(keep, swap(give, "c", 1))
    spread = lax.all_to_all(chip_sum, CHIPS, split_axis=0, concat_axis=0, tiled=True)
    block_out = (residual_slice + jnp.sum(spread.astype(F32), axis=0)).astype(BF16).T
    window_out = window_next.reshape(taps - 2, 1, own, conv_width).transpose(2, 0, 1, 3)
    return (block_out, state_next, window_out)


def solution(mesh):
    fine = Mesh(mesh.devices.reshape(4, 2, 4, 2, 2), ("x", "yh", "z", "yl", "c"))
    placed = (
        P(),
        P(),
        P(),
        P(),
        P(HEAD, None, GRP),
        P(HEAD, None, GRP),
        P(HEAD, GRP),
        P(GRP),
        P(GRP),
        P(GRP),
        P(None, GRP, None),
        P(HEAD, None, GRP, None),
        P(HEAD, GRP, None, None),
        P(GRP, None),
        P(GRP, None, HEAD),
        P(),
        P(None, GRP + HEAD),
        P(GRP + HEAD, None),
    )
    return jax.shard_map(
        local,
        mesh=fine,
        in_specs=placed,
        out_specs=(
            P(None, GRP + HEAD),
            P(HEAD, GRP, None, None),
            P(HEAD, None, GRP, None),
        ),
        check_vma=False,
    )
```

```python
import functools

import jax
import jax.numpy as jnp
from jax import lax
from jax.experimental import pallas as pl
from jax.experimental.pallas import tpu as pltpu
from jax.sharding import Mesh, PartitionSpec as P

EPS = 1e-05
GRP = ("x", "yh")
HEAD = ("z", "yl", "c")
CHIPS = ("x", "yh", "z", "yl")
NEAR = ("z", "yl")
F32 = jnp.float32
BF16 = jnp.bfloat16
HBM = pl.BlockSpec(memory_space=pltpu.HBM)
ANY = pl.BlockSpec(memory_space=pl.ANY)
VMEM = pl.BlockSpec(memory_space=pltpu.VMEM)
LANES = 128
PREP = 20
FFN = 8
FETCH = 8


def swap(value, axis, bit):
    size = lax.axis_size(axis)
    return lax.ppermute(value, axis, [(i, i ^ bit) for i in range(size)])


def add(left, right):
    return (left.astype(F32) + right.astype(F32)).astype(BF16)


def in_hbm(value):
    return pltpu.with_memory_space_constraint(value, pltpu.HBM)


def params(mib):
    return pltpu.CompilerParams(vmem_limit_bytes=mib << 20)


def contract(left, right, left_dim, right_dim):
    return lax.dot_general(
        left, right, (((left_dim,), (right_dim,)), ((), ())), preferred_element_type=F32
    )


def split3(values):
    high = values.astype(BF16)
    rest = values - high.astype(F32)
    middle = rest.astype(BF16)
    low = (rest - middle.astype(F32)).astype(BF16)
    return high, middle, low


def project_kernel(
    owner,
    history,
    hidden,
    gain,
    weights,
    select,
    step,
    keep,
    give,
    order,
    past,
    base,
    held,
    owner_held,
    history_held,
    gain_held,
    gains,
    tiles,
    select_held,
    step_held,
    sems,
    own_sem,
    small_sems,
):
    head = lax.axis_index(HEAD)
    core = lax.axis_index("c")
    count, part = tiles.shape[:2]
    rows, width = hidden.shape
    own_rows = rows * part // width
    half = rows // 2
    smalls = [
        pltpu.make_async_copy(source, target, small_sems.at[i])
        for i, (source, target) in enumerate(
            (
                (owner, owner_held),
                (history, history_held),
                (gain, gain_held),
                (select, select_held),
                (step, step_held),
            )
        )
    ]
    own_load = pltpu.make_async_copy(
        hidden.at[:, pl.ds(pl.multiple_of(head * part, part), part)], held, own_sem
    )
    copies = [
        pltpu.make_async_copy(weights.at[:, i], tiles.at[i], sems.at[i]) for i in range(count)
    ]
    for copy in smalls[:3] + [own_load] + copies + smalls[3:]:
        copy.start()
    for copy in smalls[:3]:
        copy.wait()
    gains[...] = gain_held[...].astype(F32)
    position = lax.broadcasted_iota(jnp.int32, (rows, rows), 1)
    key = (owner_held[...] * rows + position).astype(F32)
    before = (key.T < key).astype(F32)
    rank = jnp.sum(before, axis=0, keepdims=True)
    slot = lax.broadcasted_iota(jnp.int32, (rows, rows), 0)
    to_slot = jnp.where(rank == slot.astype(F32), 1.0, 0.0)
    slot_history = jnp.sum(to_slot * history_held[...].astype(F32), axis=1, keepdims=True)
    past[...] = jnp.broadcast_to(slot_history, (rows, LANES))
    near = slot < half
    inner = jnp.where(near, slot, slot - half)
    shift = jnp.where(near, core, 1 - core) * own_rows
    sent = (inner // own_rows) * (2 * own_rows) + lax.rem(inner, own_rows) + shift
    ordering = jnp.where(rank == sent.astype(F32), 1.0, 0.0).astype(BF16)
    order[...] = ordering
    source = lax.broadcasted_iota(jnp.int32, (LANES, 2 * LANES), 0)
    target = lax.broadcasted_iota(jnp.int32, (LANES, 2 * LANES), 1)
    spread = jnp.where(target == 2 * source, 1.0, 0.0).astype(BF16)
    lanes = part // LANES
    gain_row = jnp.concatenate(
        [gains[pl.ds(head * lanes + q, 1), :] for q in range(lanes)], axis=1
    )
    own_load.wait()
    base[...] = held[...]
    ordered = jnp.dot(ordering, held[...], preferred_element_type=F32)
    squares = jnp.sum(ordered * ordered, axis=1, keepdims=True)
    plain = (ordered * gain_row).astype(BF16)
    even = jnp.concatenate(
        [
            jnp.dot(plain[:, q * LANES : (q + 1) * LANES], spread, preferred_element_type=F32)
            for q in range(lanes)
        ],
        axis=1,
    )
    odd = pltpu.roll(even, 1, axis=1)
    left = jnp.concatenate([even.astype(BF16), odd.astype(BF16)], axis=0)

    def put(at, values):
        width = values.shape[1]
        for out, part in ((keep, values[:half]), (give, values[half:])):
            out[:, at : at + width] = part.astype(BF16)

    for i in range(0, count, 2):
        copies[i].wait()
        copies[i + 1].wait()
        right = jnp.concatenate(
            [tiles.at[i + k].reshape(2 * part, LANES)[...] for k in range(2)], axis=1
        )
        both = jnp.dot(left, right, preferred_element_type=F32)
        put(i * LANES, both[:rows])
        put((count + i) * LANES, both[rows:])
    for copy in smalls[3:]:
        copy.wait()
    both = jnp.dot(left, select_held[...], preferred_element_type=F32)
    at = 2 * count * LANES
    put(at, both[:rows])
    put(at + LANES, both[rows:])
    steps = contract(plain, step_held[...], 1, 1)
    missing = LANES - steps.shape[1] - 1
    put(at + 2 * LANES, jnp.concatenate([steps, squares, jnp.zeros((rows, missing), F32)], axis=1))


def mixer_kernel(
    model,
    pieces,
    past,
    window,
    taps,
    bias,
    decay_log,
    skip,
    gain,
    state,
    mixed,
    window_next,
    inputs_step,
    in_coef,
    decay,
):
    senders, own, _ = pieces.shape
    channels = mixed.shape[1]
    heads = bias.shape[1]
    width = channels // heads
    total = pieces[0].astype(F32)
    for i in range(1, senders):
        total += pieces[i].astype(F32)
    at = 2 * channels + 2 * LANES + heads
    total = total * lax.rsqrt(total[:, at : at + 1] / model + EPS)
    gate = total[:, :channels]
    fresh = total[:, channels : 2 * channels + 2 * LANES].astype(BF16).astype(F32)
    step_raw = total[:, 2 * channels + 2 * LANES : 2 * channels + 2 * LANES + heads]
    valid = past[pl.ds(pl.multiple_of(lax.axis_index(HEAD) * own, own), own), 0:1]
    lags = window.shape[0]
    entries = []
    for k in range(lags):
        mask = jnp.where(valid >= lags - k, 1.0, 0.0)
        entries.append(window[k].astype(F32) * mask)
    entries.append(fresh)
    weights = taps[...].astype(F32)
    conv = weights[lags + 1 : lags + 2]
    for k in range(lags + 1):
        conv = conv + entries[k] * weights[k : k + 1]
    for k in range(lags):
        window_next[k] = entries[k + 1].astype(BF16)
    active = conv * (1.0 / (1.0 + jnp.exp(-conv)))
    u = active[:, :channels]
    b = active[:, channels : channels + LANES]
    c = active[:, channels + LANES :]
    shifted = step_raw + bias[...]
    step = jnp.maximum(shifted, 0.0) + jnp.log1p(jnp.exp(-jnp.abs(shifted)))
    rate = jnp.exp(-step * jnp.exp(decay_log[...]))
    both = jnp.sum(b * c, axis=1, keepdims=True)
    direct = step * both + skip[...]
    head_of = lax.broadcasted_iota(jnp.int32, (heads, channels), 0)
    channel = lax.broadcasted_iota(jnp.int32, (heads, channels), 1)
    first = head_of * width
    spread = jnp.where((channel >= first) & (channel < first + width), 1.0, 0.0).astype(BF16)
    stacked = jnp.concatenate([rate, step, direct], axis=0)
    wide = sum(jnp.dot(part, spread, preferred_element_type=F32) for part in split3(stacked))
    rate_wide = wide[:own]
    step_wide = wide[own : 2 * own]
    direct_wide = wide[2 * own :]
    inputs_step[...] = step_wide * u
    in_coef[...] = b
    decay[...] = rate
    c_high = c.astype(BF16)
    c_low = (c - c_high.astype(F32)).astype(BF16)
    coefs = jnp.concatenate([c_high, c_low], axis=0)
    row = lax.broadcasted_iota(jnp.int32, (own, channels), 0)
    read = jnp.zeros((own, channels), F32)
    for s in range(own):
        found = contract(coefs, state[s], 1, 1)
        read = jnp.where(row == s, found[:own] + found[own:], read)
    gated = (rate_wide * read + direct_wide * u) * (gate * (1.0 / (1.0 + jnp.exp(-gate))))
    scale = lax.rsqrt(jnp.sum(gated * gated, axis=1, keepdims=True) / channels + EPS)
    mixed[...] = (gated * scale * gain[...].astype(F32)).astype(BF16)


def add_kernel(left, right, out):
    for i in range(out.shape[0]):
        out[i] = (left[i].astype(F32) + right[i].astype(F32)).astype(BF16)


def residual_kernel(mixed, other, order, base, out):
    total = (mixed[...].astype(F32) + other[...].astype(F32)).astype(BF16)
    piece = (base[...].astype(F32) + contract(order[...], total, 0, 0)).astype(BF16)
    for i in range(out.shape[0]):
        out[i] = piece


def fetch_kernel(after, source, out, sem):
    copy = pltpu.make_async_copy(source, out, sem)
    copy.start()
    copy.wait()


def fetch(after, source):
    return pl.pallas_call(
        fetch_kernel,
        out_shape=pltpu.VMEM(source.shape, source.dtype),
        in_specs=[ANY, HBM],
        out_specs=VMEM,
        scratch_shapes=[pltpu.SemaphoreType.DMA],
        compiler_params=params(FETCH),
        cost_estimate=pl.CostEstimate(
            flops=0, bytes_accessed=2 * source.size * source.dtype.itemsize, transcendentals=0
        ),
    )(after, in_hbm(source))


def ffn_kernel(
    near,
    far,
    gain,
    up,
    down,
    keep,
    give,
    slice_out,
    turned,
    gains,
):
    core = lax.axis_index("c")
    flat = lax.axis_index(GRP + HEAD)
    chunks, rows, part = near.shape
    hidden = up.shape[2]
    model = 2 * chunks * part
    piece = keep.shape[1]
    turns = [(j, which) for which in range(2) for j in range(chunks)]
    gains[...] = gain[...].astype(F32)
    squares = jnp.zeros((rows, LANES), F32)
    total = jnp.zeros((rows, hidden), F32)
    lanes = part // LANES
    for k, (j, which) in enumerate(turns):
        source = near if which == 0 else far
        at = 2 * j + (core if which == 0 else 1 - core)
        scaled = []
        for q in range(lanes):
            chunk = source[j, :, q * LANES : (q + 1) * LANES].astype(F32)
            squares += chunk * chunk
            row = gains[pl.ds(at * lanes + q, 1), :]
            scaled.append((chunk * row).astype(BF16))
        total += jnp.dot(jnp.concatenate(scaled, axis=1), up[at], preferred_element_type=F32)
    scale = lax.rsqrt(jnp.sum(squares, axis=1, keepdims=True) / model + EPS)
    raised = jnp.maximum(total * scale, 0.0)
    squared = (raised * raised).astype(BF16)
    per_part = part // piece
    owner = flat // per_part
    mine = near[owner // 2].astype(F32)
    other = far[owner // 2].astype(F32)
    turned[...] = jnp.where(lax.rem(owner, 2) == core, mine, other).T
    slice_out[...] = turned[pl.ds(pl.multiple_of(lax.rem(flat, per_part) * piece, piece), piece), :]
    for k in range(2 * chunks):
        right = down[:, k * part : (k + 1) * part]
        out = jnp.dot(squared, right, preferred_element_type=F32).astype(BF16).T
        for q in range(part // (2 * piece)):
            low = out[2 * q * piece : (2 * q + 1) * piece]
            high = out[(2 * q + 1) * piece : (2 * q + 2) * piece]
            chip = k * (part // (2 * piece)) + q
            keep[chip] = jnp.where(core == 0, low, high)
            give[chip] = jnp.where(core == 0, high, low)


def local(
    hidden_in,
    row_owner,
    history_len,
    pre_gain,
    inner_proj,
    select_proj,
    step_proj,
    step_bias,
    decay_log,
    skip_gain,
    conv_taps,
    conv_window,
    state_cache,
    mixer_gain,
    output_proj,
    channel_gain,
    up_weight,
    down_weight,
):
    rows, model = hidden_in.shape
    heads_axis = lax.axis_size(HEAD)
    groups_axis = lax.axis_size(GRP)
    own = rows // heads_axis
    part = model // heads_axis
    channels = mixer_gain.shape[1]
    heads = step_proj.shape[1]
    state_size = state_cache.shape[3]
    head_width = state_cache.shape[2]
    taps = conv_taps.shape[0]
    conv_width = conv_taps.shape[2]
    hidden_units = up_weight.shape[1]
    tile_count = channels // LANES
    head_index = lax.axis_index(HEAD)
    shape = jax.ShapeDtypeStruct

    tiled = inner_proj.reshape(part, 2, tile_count, LANES).transpose(0, 2, 1, 3)
    sent_width = 2 * channels + 2 * state_size + LANES
    near_owners = heads_axis // 2
    keep, give, order, past, base = pl.pallas_call(
        project_kernel,
        out_shape=(
            pltpu.VMEM((rows // 2, sent_width), BF16),
            pltpu.VMEM((rows // 2, sent_width), BF16),
            shape((rows, rows), BF16),
            pltpu.VMEM((rows, LANES), F32),
            shape((rows, part), BF16),
        ),
        in_specs=[HBM] * 7,
        out_specs=(VMEM,) * 5,
        scratch_shapes=[
            pltpu.VMEM((rows, part), BF16),
            pltpu.VMEM((1, rows), jnp.int32),
            pltpu.VMEM((1, rows), jnp.int32),
            pltpu.VMEM((model // LANES, LANES), BF16),
            pltpu.VMEM((model // LANES, LANES), F32),
            pltpu.VMEM((tile_count, part, 2, LANES), BF16),
            pltpu.VMEM((2 * part, state_size), BF16),
            pltpu.VMEM((heads, part), BF16),
            pltpu.SemaphoreType.DMA((tile_count,)),
            pltpu.SemaphoreType.DMA,
            pltpu.SemaphoreType.DMA((5,)),
        ],
        compiler_params=params(PREP),
    )(
        *(
            in_hbm(value)
            for value in (
                row_owner.reshape(1, rows),
                history_len.reshape(1, rows),
                hidden_in,
                pre_gain.reshape(model // LANES, LANES),
                tiled,
                select_proj.reshape(2 * part, state_size),
                step_proj.T,
            )
        )
    )
    keep, give = (value.reshape(near_owners, own, sent_width) for value in (keep, give))
    chip_terms = add(keep, swap(give, "c", 1))
    pieces = lax.all_to_all(chip_terms, NEAR, split_axis=0, concat_axis=0, tiled=True)
    mixed_own, window_next, inputs_step, in_coef, decay = pl.pallas_call(
        functools.partial(mixer_kernel, model),
        out_shape=(
            shape((own, channels), BF16),
            shape((taps - 2, own, conv_width), BF16),
            shape((own, channels), F32),
            shape((own, state_size), F32),
            shape((own, heads), F32),
        ),
        in_specs=[VMEM] * 9,
        out_specs=(VMEM,) * 5,
        compiler_params=params(16),
    )(
        pieces,
        past,
        conv_window.transpose(1, 2, 0, 3).reshape(taps - 2, own, conv_width),
        conv_taps.reshape(taps, conv_width),
        step_bias.reshape(1, heads),
        decay_log.reshape(1, heads),
        skip_gain.reshape(1, heads),
        mixer_gain,
        state_cache.reshape(own, heads * head_width, state_size),
    )
    near_mix = lax.all_to_all(
        jnp.broadcast_to(mixed_own[None], (near_owners, own, channels)),
        NEAR,
        split_axis=0,
        concat_axis=0,
        tiled=True,
    )
    near_mix, inputs_step, in_coef, decay = lax.optimization_barrier(
        (near_mix, inputs_step, in_coef, decay)
    )
    far_mix = swap(near_mix, "c", 1)
    out_weight = output_proj.reshape(channels, part)
    mixed = jnp.concatenate(
        [
            jnp.dot(mix.reshape(rows // 2, channels), out_weight, preferred_element_type=F32)
            for mix in (near_mix, far_mix)
        ]
    ).astype(BF16)
    step_input = inputs_step.reshape(own, heads, head_width)
    state_next = (
        decay[..., None, None] * state_cache.astype(F32)
        + step_input[..., None] * in_coef[:, None, None, :]
    ).astype(BF16)
    for bit in (1, 3):
        other = swap(mixed, "x", bit)
        if bit == 1:
            other, state_next = lax.optimization_barrier((other, state_next))
        mixed = add(mixed, other)
    other = swap(mixed, "yh", 1)
    down_near = fetch(mixed, down_weight)
    other, down_near = lax.optimization_barrier((other, down_near))
    spread_piece = pl.pallas_call(
        residual_kernel,
        out_shape=shape((near_owners, rows, part), BF16),
        in_specs=[VMEM] * 4,
        out_specs=VMEM,
        compiler_params=params(4),
    )(mixed, other, order, base)
    near = lax.all_to_all(spread_piece, NEAR, split_axis=0, concat_axis=0, tiled=True)
    far = swap(near, "c", 1)
    up_near = fetch(near, up_weight.reshape(heads_axis, part, hidden_units))
    far, up_near = lax.optimization_barrier((far, up_near))
    chips = groups_axis * heads_axis // 2
    piece = model // (groups_axis * heads_axis)
    keep, give, residual_slice = pl.pallas_call(
        ffn_kernel,
        out_shape=(
            shape((chips, piece, rows), BF16),
            shape((chips, piece, rows), BF16),
            shape((piece, rows), F32),
        ),
        in_specs=[VMEM] * 5,
        out_specs=(VMEM,) * 3,
        scratch_shapes=[
            pltpu.VMEM((part, rows), F32),
            pltpu.VMEM((model // LANES, LANES), F32),
        ],
        compiler_params=params(FFN),
    )(
        near,
        far,
        channel_gain.reshape(model // LANES, LANES),
        up_near,
        down_near,
    )
    chip_sum = pl.pallas_call(
        add_kernel,
        out_shape=pltpu.VMEM(keep.shape, BF16),
        in_specs=[VMEM] * 2,
        out_specs=VMEM,
        compiler_params=params(4),
    )(keep, swap(give, "c", 1))
    spread = lax.all_to_all(chip_sum, CHIPS, split_axis=0, concat_axis=0, tiled=True)
    block_out = (residual_slice + jnp.sum(spread.astype(F32), axis=0)).astype(BF16).T
    window_out = window_next.reshape(taps - 2, 1, own, conv_width).transpose(2, 0, 1, 3)
    return (block_out, state_next, window_out)


def solution(mesh):
    fine = Mesh(mesh.devices.reshape(4, 2, 4, 2, 2), ("x", "yh", "z", "yl", "c"))
    placed = (
        P(),
        P(),
        P(),
        P(),
        P(HEAD, None, GRP),
        P(HEAD, None, GRP),
        P(HEAD, GRP),
        P(GRP),
        P(GRP),
        P(GRP),
        P(None, GRP, None),
        P(HEAD, None, GRP, None),
        P(HEAD, GRP, None, None),
        P(GRP, None),
        P(GRP, None, HEAD),
        P(),
        P(None, GRP + HEAD),
        P(GRP + HEAD, None),
    )
    return jax.shard_map(
        local,
        mesh=fine,
        in_specs=placed,
        out_specs=(
            P(None, GRP + HEAD),
            P(HEAD, GRP, None, None),
            P(HEAD, None, GRP, None),
        ),
        check_vma=False,
    )
```

```python
import functools

import jax
import jax.numpy as jnp
from jax import lax
from jax.experimental import pallas as pl
from jax.experimental.pallas import tpu as pltpu
from jax.sharding import Mesh, PartitionSpec as P

EPS = 1e-05
GRP = ("x", "yh")
HEAD = ("z", "yl", "c")
CHIPS = ("x", "yh", "z", "yl")
NEAR = ("z", "yl")
F32 = jnp.float32
BF16 = jnp.bfloat16
HBM = pl.BlockSpec(memory_space=pltpu.HBM)
ANY = pl.BlockSpec(memory_space=pl.ANY)
VMEM = pl.BlockSpec(memory_space=pltpu.VMEM)
LANES = 128
PREP = 20
FFN = 8
FETCH = 8


def swap(value, axis, bit):
    size = lax.axis_size(axis)
    return lax.ppermute(value, axis, [(i, i ^ bit) for i in range(size)])


def add(left, right):
    return (left.astype(F32) + right.astype(F32)).astype(BF16)


def in_hbm(value):
    return pltpu.with_memory_space_constraint(value, pltpu.HBM)


def params(mib):
    return pltpu.CompilerParams(vmem_limit_bytes=mib << 20)


def contract(left, right, left_dim, right_dim):
    return lax.dot_general(
        left, right, (((left_dim,), (right_dim,)), ((), ())), preferred_element_type=F32
    )


def split3(values):
    high = values.astype(BF16)
    rest = values - high.astype(F32)
    middle = rest.astype(BF16)
    low = (rest - middle.astype(F32)).astype(BF16)
    return high, middle, low


def project_kernel(
    owner,
    history,
    hidden,
    gain,
    weights,
    select,
    step,
    far_tail,
    far_left,
    near_tail,
    near_left,
    tiles,
    order,
    past,
    base,
    held,
    owner_held,
    history_held,
    gain_held,
    gains,
    select_held,
    step_held,
    sems,
    own_sem,
    small_sems,
):
    head = lax.axis_index(HEAD)
    core = lax.axis_index("c")
    count, part = tiles.shape[:2]
    rows, width = hidden.shape
    own_rows = rows * part // width
    half = rows // 2
    smalls = [
        pltpu.make_async_copy(source, target, small_sems.at[i])
        for i, (source, target) in enumerate(
            (
                (owner, owner_held),
                (history, history_held),
                (gain, gain_held),
                (select, select_held),
                (step, step_held),
            )
        )
    ]
    own_load = pltpu.make_async_copy(
        hidden.at[:, pl.ds(pl.multiple_of(head * part, part), part)], held, own_sem
    )
    copies = [
        pltpu.make_async_copy(weights.at[:, i], tiles.at[i], sems.at[i]) for i in range(count)
    ]
    for copy in smalls[:3] + [own_load] + copies + smalls[3:]:
        copy.start()
    for copy in smalls[:3]:
        copy.wait()
    gains[...] = gain_held[...].astype(F32)
    position = lax.broadcasted_iota(jnp.int32, (rows, rows), 1)
    key = (owner_held[...] * rows + position).astype(F32)
    before = (key.T < key).astype(F32)
    rank = jnp.sum(before, axis=0, keepdims=True)
    slot = lax.broadcasted_iota(jnp.int32, (rows, rows), 0)
    to_slot = jnp.where(rank == slot.astype(F32), 1.0, 0.0)
    slot_history = jnp.sum(to_slot * history_held[...].astype(F32), axis=1, keepdims=True)
    past[...] = jnp.broadcast_to(slot_history, (rows, LANES))
    near = slot < half
    inner = jnp.where(near, slot, slot - half)
    shift = jnp.where(near, core, 1 - core) * own_rows
    sent = (inner // own_rows) * (2 * own_rows) + lax.rem(inner, own_rows) + shift
    ordering = jnp.where(rank == sent.astype(F32), 1.0, 0.0).astype(BF16)
    order[...] = ordering
    source = lax.broadcasted_iota(jnp.int32, (LANES, 2 * LANES), 0)
    target = lax.broadcasted_iota(jnp.int32, (LANES, 2 * LANES), 1)
    spread = jnp.where(target == 2 * source, 1.0, 0.0).astype(BF16)
    lanes = part // LANES
    gain_row = jnp.concatenate(
        [gains[pl.ds(head * lanes + q, 1), :] for q in range(lanes)], axis=1
    )
    own_load.wait()
    base[...] = held[...]
    ordered = jnp.dot(ordering, held[...], preferred_element_type=F32)
    squares = jnp.sum(ordered * ordered, axis=1, keepdims=True)
    plain = (ordered * gain_row).astype(BF16)
    even = jnp.concatenate(
        [
            jnp.dot(plain[:, q * LANES : (q + 1) * LANES], spread, preferred_element_type=F32)
            for q in range(lanes)
        ],
        axis=1,
    )
    odd = pltpu.roll(even, 1, axis=1)
    even, odd = even.astype(BF16), odd.astype(BF16)
    near_left[...] = jnp.concatenate([even[:half], odd[:half]], axis=0)
    far_left[...] = jnp.concatenate([even[half:], odd[half:]], axis=0)
    for copy in smalls[3:]:
        copy.wait()
    steps = contract(plain, step_held[...], 1, 1)
    missing = LANES - steps.shape[1] - 1
    steps = jnp.concatenate([steps, squares, jnp.zeros((rows, missing), F32)], axis=1)
    for out, left, part_steps in (
        (near_tail, near_left, steps[:half]),
        (far_tail, far_left, steps[half:]),
    ):
        both = jnp.dot(left[...], select_held[...], preferred_element_type=F32)
        out[:, :LANES] = both[:half].astype(BF16)
        out[:, LANES : 2 * LANES] = both[half:].astype(BF16)
        out[:, 2 * LANES :] = part_steps.astype(BF16)
    for copy in copies:
        copy.wait()


def half_kernel(left, tiles, tail, out):
    count = tiles.shape[0]
    half = out.shape[0]
    for i in range(0, count, 2):
        right = jnp.concatenate([tiles[i], tiles[i + 1]], axis=1)
        both = jnp.dot(left[...], right, preferred_element_type=F32)
        out[:, i * LANES : (i + 2) * LANES] = both[:half].astype(BF16)
        out[:, (count + i) * LANES : (count + i + 2) * LANES] = both[half:].astype(BF16)
    out[:, 2 * count * LANES :] = tail[...]


def mixer_kernel(
    model,
    pieces,
    past,
    window,
    taps,
    bias,
    decay_log,
    skip,
    gain,
    state,
    mixed,
    window_next,
    inputs_step,
    in_coef,
    decay,
):
    senders, own, _ = pieces.shape
    channels = mixed.shape[1]
    heads = bias.shape[1]
    width = channels // heads
    total = pieces[0].astype(F32)
    for i in range(1, senders):
        total += pieces[i].astype(F32)
    at = 2 * channels + 2 * LANES + heads
    total = total * lax.rsqrt(total[:, at : at + 1] / model + EPS)
    gate = total[:, :channels]
    fresh = total[:, channels : 2 * channels + 2 * LANES].astype(BF16).astype(F32)
    step_raw = total[:, 2 * channels + 2 * LANES : 2 * channels + 2 * LANES + heads]
    valid = past[pl.ds(pl.multiple_of(lax.axis_index(HEAD) * own, own), own), 0:1]
    lags = window.shape[0]
    entries = []
    for k in range(lags):
        mask = jnp.where(valid >= lags - k, 1.0, 0.0)
        entries.append(window[k].astype(F32) * mask)
    entries.append(fresh)
    weights = taps[...].astype(F32)
    conv = weights[lags + 1 : lags + 2]
    for k in range(lags + 1):
        conv = conv + entries[k] * weights[k : k + 1]
    for k in range(lags):
        window_next[k] = entries[k + 1].astype(BF16)
    active = conv * (1.0 / (1.0 + jnp.exp(-conv)))
    u = active[:, :channels]
    b = active[:, channels : channels + LANES]
    c = active[:, channels + LANES :]
    shifted = step_raw + bias[...]
    step = jnp.maximum(shifted, 0.0) + jnp.log1p(jnp.exp(-jnp.abs(shifted)))
    rate = jnp.exp(-step * jnp.exp(decay_log[...]))
    both = jnp.sum(b * c, axis=1, keepdims=True)
    direct = step * both + skip[...]
    head_of = lax.broadcasted_iota(jnp.int32, (heads, channels), 0)
    channel = lax.broadcasted_iota(jnp.int32, (heads, channels), 1)
    first = head_of * width
    spread = jnp.where((channel >= first) & (channel < first + width), 1.0, 0.0).astype(BF16)
    stacked = jnp.concatenate([rate, step, direct], axis=0)
    wide = sum(jnp.dot(part, spread, preferred_element_type=F32) for part in split3(stacked))
    rate_wide = wide[:own]
    step_wide = wide[own : 2 * own]
    direct_wide = wide[2 * own :]
    inputs_step[...] = step_wide * u
    in_coef[...] = b
    decay[...] = rate
    c_high = c.astype(BF16)
    c_low = (c - c_high.astype(F32)).astype(BF16)
    coefs = jnp.concatenate([c_high, c_low], axis=0)
    row = lax.broadcasted_iota(jnp.int32, (own, channels), 0)
    read = jnp.zeros((own, channels), F32)
    for s in range(own):
        found = contract(coefs, state[s], 1, 1)
        read = jnp.where(row == s, found[:own] + found[own:], read)
    gated = (rate_wide * read + direct_wide * u) * (gate * (1.0 / (1.0 + jnp.exp(-gate))))
    scale = lax.rsqrt(jnp.sum(gated * gated, axis=1, keepdims=True) / channels + EPS)
    mixed[...] = (gated * scale * gain[...].astype(F32)).astype(BF16)


def add_kernel(left, right, out):
    for i in range(out.shape[0]):
        out[i] = (left[i].astype(F32) + right[i].astype(F32)).astype(BF16)


def residual_kernel(mixed, other, order, base, out):
    total = (mixed[...].astype(F32) + other[...].astype(F32)).astype(BF16)
    piece = (base[...].astype(F32) + contract(order[...], total, 0, 0)).astype(BF16)
    for i in range(out.shape[0]):
        out[i] = piece


def fetch_kernel(after, source, out, sem):
    copy = pltpu.make_async_copy(source, out, sem)
    copy.start()
    copy.wait()


def fetch(after, source):
    return pl.pallas_call(
        fetch_kernel,
        out_shape=pltpu.VMEM(source.shape, source.dtype),
        in_specs=[ANY, HBM],
        out_specs=VMEM,
        scratch_shapes=[pltpu.SemaphoreType.DMA],
        compiler_params=params(FETCH),
        cost_estimate=pl.CostEstimate(
            flops=0, bytes_accessed=2 * source.size * source.dtype.itemsize, transcendentals=0
        ),
    )(after, in_hbm(source))


def ffn_kernel(
    near,
    far,
    gain,
    up,
    down,
    keep,
    give,
    slice_out,
    turned,
    gains,
):
    core = lax.axis_index("c")
    flat = lax.axis_index(GRP + HEAD)
    chunks, rows, part = near.shape
    hidden = up.shape[2]
    model = 2 * chunks * part
    piece = keep.shape[1]
    turns = [(j, which) for which in range(2) for j in range(chunks)]
    gains[...] = gain[...].astype(F32)
    squares = jnp.zeros((rows, LANES), F32)
    total = jnp.zeros((rows, hidden), F32)
    lanes = part // LANES
    for k, (j, which) in enumerate(turns):
        source = near if which == 0 else far
        at = 2 * j + (core if which == 0 else 1 - core)
        scaled = []
        for q in range(lanes):
            chunk = source[j, :, q * LANES : (q + 1) * LANES].astype(F32)
            squares += chunk * chunk
            row = gains[pl.ds(at * lanes + q, 1), :]
            scaled.append((chunk * row).astype(BF16))
        total += jnp.dot(jnp.concatenate(scaled, axis=1), up[at], preferred_element_type=F32)
    scale = lax.rsqrt(jnp.sum(squares, axis=1, keepdims=True) / model + EPS)
    raised = jnp.maximum(total * scale, 0.0)
    squared = (raised * raised).astype(BF16)
    per_part = part // piece
    owner = flat // per_part
    mine = near[owner // 2].astype(F32)
    other = far[owner // 2].astype(F32)
    turned[...] = jnp.where(lax.rem(owner, 2) == core, mine, other).T
    slice_out[...] = turned[pl.ds(pl.multiple_of(lax.rem(flat, per_part) * piece, piece), piece), :]
    for k in range(2 * chunks):
        right = down[:, k * part : (k + 1) * part]
        out = jnp.dot(squared, right, preferred_element_type=F32).astype(BF16).T
        for q in range(part // (2 * piece)):
            low = out[2 * q * piece : (2 * q + 1) * piece]
            high = out[(2 * q + 1) * piece : (2 * q + 2) * piece]
            chip = k * (part // (2 * piece)) + q
            keep[chip] = jnp.where(core == 0, low, high)
            give[chip] = jnp.where(core == 0, high, low)


def local(
    hidden_in,
    row_owner,
    history_len,
    pre_gain,
    inner_proj,
    select_proj,
    step_proj,
    step_bias,
    decay_log,
    skip_gain,
    conv_taps,
    conv_window,
    state_cache,
    mixer_gain,
    output_proj,
    channel_gain,
    up_weight,
    down_weight,
):
    rows, model = hidden_in.shape
    heads_axis = lax.axis_size(HEAD)
    groups_axis = lax.axis_size(GRP)
    own = rows // heads_axis
    part = model // heads_axis
    channels = mixer_gain.shape[1]
    heads = step_proj.shape[1]
    state_size = state_cache.shape[3]
    head_width = state_cache.shape[2]
    taps = conv_taps.shape[0]
    conv_width = conv_taps.shape[2]
    hidden_units = up_weight.shape[1]
    tile_count = channels // LANES
    head_index = lax.axis_index(HEAD)
    shape = jax.ShapeDtypeStruct

    tiled = inner_proj.reshape(part, 2, tile_count, LANES).transpose(0, 2, 1, 3)
    sent_width = 2 * channels + 2 * state_size + LANES
    near_owners = heads_axis // 2
    far_tail, far_left, near_tail, near_left, tiles, order, past, base = pl.pallas_call(
        project_kernel,
        out_shape=(
            pltpu.VMEM((rows // 2, sent_width - 2 * channels), BF16),
            pltpu.VMEM((rows, 2 * part), BF16),
            pltpu.VMEM((rows // 2, sent_width - 2 * channels), BF16),
            pltpu.VMEM((rows, 2 * part), BF16),
            pltpu.VMEM((tile_count, part, 2, LANES), BF16),
            shape((rows, rows), BF16),
            pltpu.VMEM((rows, LANES), F32),
            shape((rows, part), BF16),
        ),
        in_specs=[HBM] * 7,
        out_specs=(VMEM,) * 8,
        scratch_shapes=[
            pltpu.VMEM((rows, part), BF16),
            pltpu.VMEM((1, rows), jnp.int32),
            pltpu.VMEM((1, rows), jnp.int32),
            pltpu.VMEM((model // LANES, LANES), BF16),
            pltpu.VMEM((model // LANES, LANES), F32),
            pltpu.VMEM((2 * part, state_size), BF16),
            pltpu.VMEM((heads, part), BF16),
            pltpu.SemaphoreType.DMA((tile_count,)),
            pltpu.SemaphoreType.DMA,
            pltpu.SemaphoreType.DMA((5,)),
        ],
        compiler_params=params(PREP),
    )(
        *(
            in_hbm(value)
            for value in (
                row_owner.reshape(1, rows),
                history_len.reshape(1, rows),
                hidden_in,
                pre_gain.reshape(model // LANES, LANES),
                tiled,
                select_proj.reshape(2 * part, state_size),
                step_proj.T,
            )
        )
    )
    half_call = pl.pallas_call(
        half_kernel,
        out_shape=pltpu.VMEM((rows // 2, sent_width), BF16),
        in_specs=[VMEM] * 3,
        out_specs=VMEM,
        compiler_params=params(8),
        cost_estimate=pl.CostEstimate(
            flops=8 * rows * part * channels, bytes_accessed=8 * part * channels, transcendentals=0
        ),
    )
    tiles = tiles.reshape(tile_count, 2 * part, LANES)
    give = half_call(far_left, tiles, far_tail)
    keep = half_call(near_left, tiles, near_tail)
    keep, give = (value.reshape(near_owners, own, sent_width) for value in (keep, give))
    chip_terms = add(keep, swap(give, "c", 1))
    pieces = lax.all_to_all(chip_terms, NEAR, split_axis=0, concat_axis=0, tiled=True)
    mixed_own, window_next, inputs_step, in_coef, decay = pl.pallas_call(
        functools.partial(mixer_kernel, model),
        out_shape=(
            shape((own, channels), BF16),
            shape((taps - 2, own, conv_width), BF16),
            shape((own, channels), F32),
            shape((own, state_size), F32),
            shape((own, heads), F32),
        ),
        in_specs=[VMEM] * 9,
        out_specs=(VMEM,) * 5,
        compiler_params=params(16),
    )(
        pieces,
        past,
        conv_window.transpose(1, 2, 0, 3).reshape(taps - 2, own, conv_width),
        conv_taps.reshape(taps, conv_width),
        step_bias.reshape(1, heads),
        decay_log.reshape(1, heads),
        skip_gain.reshape(1, heads),
        mixer_gain,
        state_cache.reshape(own, heads * head_width, state_size),
    )
    near_mix = lax.all_to_all(
        jnp.broadcast_to(mixed_own[None], (near_owners, own, channels)),
        NEAR,
        split_axis=0,
        concat_axis=0,
        tiled=True,
    )
    near_mix, inputs_step, in_coef, decay = lax.optimization_barrier(
        (near_mix, inputs_step, in_coef, decay)
    )
    far_mix = swap(near_mix, "c", 1)
    out_weight = output_proj.reshape(channels, part)
    mixed = jnp.concatenate(
        [
            jnp.dot(mix.reshape(rows // 2, channels), out_weight, preferred_element_type=F32)
            for mix in (near_mix, far_mix)
        ]
    ).astype(BF16)
    step_input = inputs_step.reshape(own, heads, head_width)
    state_next = (
        decay[..., None, None] * state_cache.astype(F32)
        + step_input[..., None] * in_coef[:, None, None, :]
    ).astype(BF16)
    for bit in (1, 3):
        other = swap(mixed, "x", bit)
        if bit == 1:
            other, state_next = lax.optimization_barrier((other, state_next))
        mixed = add(mixed, other)
    other = swap(mixed, "yh", 1)
    down_near = fetch(mixed, down_weight)
    other, down_near = lax.optimization_barrier((other, down_near))
    spread_piece = pl.pallas_call(
        residual_kernel,
        out_shape=shape((near_owners, rows, part), BF16),
        in_specs=[VMEM] * 4,
        out_specs=VMEM,
        compiler_params=params(4),
    )(mixed, other, order, base)
    near = lax.all_to_all(spread_piece, NEAR, split_axis=0, concat_axis=0, tiled=True)
    far = swap(near, "c", 1)
    up_near = fetch(near, up_weight.reshape(heads_axis, part, hidden_units))
    far, up_near = lax.optimization_barrier((far, up_near))
    chips = groups_axis * heads_axis // 2
    piece = model // (groups_axis * heads_axis)
    keep, give, residual_slice = pl.pallas_call(
        ffn_kernel,
        out_shape=(
            shape((chips, piece, rows), BF16),
            shape((chips, piece, rows), BF16),
            shape((piece, rows), F32),
        ),
        in_specs=[VMEM] * 5,
        out_specs=(VMEM,) * 3,
        scratch_shapes=[
            pltpu.VMEM((part, rows), F32),
            pltpu.VMEM((model // LANES, LANES), F32),
        ],
        compiler_params=params(FFN),
    )(
        near,
        far,
        channel_gain.reshape(model // LANES, LANES),
        up_near,
        down_near,
    )
    chip_sum = pl.pallas_call(
        add_kernel,
        out_shape=pltpu.VMEM(keep.shape, BF16),
        in_specs=[VMEM] * 2,
        out_specs=VMEM,
        compiler_params=params(4),
    )(keep, swap(give, "c", 1))
    spread = lax.all_to_all(chip_sum, CHIPS, split_axis=0, concat_axis=0, tiled=True)
    block_out = (residual_slice + jnp.sum(spread.astype(F32), axis=0)).astype(BF16).T
    window_out = window_next.reshape(taps - 2, 1, own, conv_width).transpose(2, 0, 1, 3)
    return (block_out, state_next, window_out)


def solution(mesh):
    fine = Mesh(mesh.devices.reshape(4, 2, 4, 2, 2), ("x", "yh", "z", "yl", "c"))
    placed = (
        P(),
        P(),
        P(),
        P(),
        P(HEAD, None, GRP),
        P(HEAD, None, GRP),
        P(HEAD, GRP),
        P(GRP),
        P(GRP),
        P(GRP),
        P(None, GRP, None),
        P(HEAD, None, GRP, None),
        P(HEAD, GRP, None, None),
        P(GRP, None),
        P(GRP, None, HEAD),
        P(),
        P(None, GRP + HEAD),
        P(GRP + HEAD, None),
    )
    return jax.shard_map(
        local,
        mesh=fine,
        in_specs=placed,
        out_specs=(
            P(None, GRP + HEAD),
            P(HEAD, GRP, None, None),
            P(HEAD, None, GRP, None),
        ),
        check_vma=False,
    )
```
